128 devices in a mesh: dev: 128 (over x, y, z, core).
Axes of the slice: x: 4, y: 4, z: 4, core: 2. Of those that a mesh axis runs over, the one named last changes fastest.
Arguments:
- object_field: float32 [2, 16384, 2048], P(None, 'dev'), may hold values from -5 to 5
- probe: float32 [2, 4, 128, 128], replicated, may hold values from -6 to 6
- amplitudes: float32 [2048, 128, 128], P('dev'), may hold values from 0.2 to 3
- positions: int32 [2048, 2], P('dev'), may hold values from 0 to 16256, as said below
- counts: int32 [128], P('dev'), may hold values from 1 to 16, as said below
Outputs:
- new_object: float32 [2, 16384, 2048], P(None, 'dev')
- new_probe: float32 [2, 4, 128, 128], replicated
The draws below stay inside these ranges and needn't reach their ends.
Inputs may be any that keep to these rules, and one draw needn't show every extreme that they name: `positions`: slot j's top row lies in the object rows of device j // 16: from (j // 16) * 128 to (j // 16) * 128 + 127, and the window stays inside the object; the left column is at most 1920. `counts`: slots of a device below its count are live, the others are ignored.
All inputs are finite; a program needn't handle non-finite values.
Results may differ from the reference program's by a relative error of at most 0.0003.
Values sent between devices are 32-bit elements; how exact they have to be, the bound alone decides.
No kernel may reach another device: no remote copies, remote signals or barrier semaphores. Data moves between devices by JAX's collectives and lax.ppermute only.
A program may use at most 128 MiB of HBM per device.

```python
import math
import jax
import jax.numpy as jnp
from jax import lax

PATCH = 128
MODES = 4
SH = 128
W = 2048
PAT_DEV = 16
ITERS = 2
NR = 16384
NPAT = 2048
N_DEV = 128


def draw_positions(key, part):
    key = jax.random.fold_in(key, 1)
    row_key, col_key = jax.random.split(key)
    slots = jnp.arange(NPAT, dtype=jnp.int32)
    owner = slots // PAT_DEV
    top = jnp.where(owner == N_DEV - 1, SH - PATCH + 1, SH)
    local = jax.random.randint(row_key, (NPAT,), 0, SH, dtype=jnp.int32) % top
    rows = owner * SH + local
    rows = rows.at[NPAT - 1].set(NR - PATCH)
    rows = rows.at[0].set(0)
    cols = jax.random.randint(col_key, (NPAT,), 0, W - PATCH + 1, dtype=jnp.int32)
    cols = cols.at[0].set(0)
    return jnp.stack([rows, cols], axis=1)


def draw_counts(key, part):
    key = jax.random.fold_in(key, 2)
    values = jax.random.randint(key, (N_DEV,), 1, PAT_DEV + 1, dtype=jnp.int32)
    return values.at[0].set(PAT_DEV)


def levels(stream_key, extent, shards, low, high):
    level, own = 1.0, jax.random.fold_in(stream_key, 6)
    for position, blocks in shards:
        steps = jnp.exp(jax.random.uniform(jax.random.fold_in(own, position), (blocks,), jnp.float32, low / len(shards), high / len(shards)))
        level = level * jnp.repeat(steps, extent[position] // blocks).reshape([-1 if axis == position else 1 for axis in range(len(extent))])
    return level


def gaussian(own_key, dims, spread, bound, shards=(), held_as=jnp.bfloat16):
    drawn = spread * jax.random.normal(own_key, dims, jnp.float32)
    if shards:
        drawn = drawn * levels(own_key, dims, shards, -0.22, 0.18)
    return jnp.clip(drawn, -bound, bound).astype(held_as)


def setup_inputs(seed: int = 0) -> dict:
    streams_of = jax.random.split(jax.random.key(seed), 6)
    return {
        "object_field": gaussian(streams_of[0], (2, NR, W), 0.7, 5.0, ((1, 128),), jnp.float32),
        "probe": gaussian(streams_of[1], (2, MODES, PATCH, PATCH), 1.0, 6.0, (), jnp.float32),
        "amplitudes": jnp.clip(jnp.exp(math.log(3.0) - 2.7080502 * jax.random.uniform(streams_of[2], (NPAT, PATCH, PATCH), jnp.float32) ** levels(streams_of[2], (NPAT, PATCH, PATCH), ((0, 128),), -0.2, 0.2)), 0.2, 3.0),
        "positions": draw_positions(jax.random.fold_in(streams_of[5], 71), 0),
        "counts": draw_counts(jax.random.fold_in(streams_of[5], 71), 0),
    }


def reference(object_field, probe, amplitudes, positions, counts):
    dense = object_field[0] + 1j * object_field[1]
    modes = probe[0] + 1j * probe[1]
    slots = jnp.arange(NPAT, dtype=jnp.int32)
    live = (slots % PAT_DEV < counts[slots // PAT_DEV]).astype(object_field.dtype)
    for step in range(ITERS):

        def visit(carry, item):
            grad_obj, illum, grad_probe, pnorm = carry
            amplitude, place, alive = item
            row = place[0].astype(jnp.int32)
            col = place[1].astype(jnp.int32)
            window = lax.dynamic_slice(dense, (row, col), (PATCH, PATCH))
            far = jnp.fft.fft2(modes * window[None], norm='ortho')
            intensity = lax.optimization_barrier(jnp.sum(far.real ** 2 + far.imag ** 2, axis=0))
            ratio = amplitude / jnp.sqrt(intensity + 0.5)
            chi = jnp.fft.ifft2(far * (alive * (1.0 - ratio))[None], norm='ortho')
            gpatch = lax.optimization_barrier(jnp.sum(jnp.conj(modes) * chi, axis=0))
            lit = alive * lax.optimization_barrier(jnp.sum(modes.real ** 2 + modes.imag ** 2, axis=0))
            old_g = lax.dynamic_slice(grad_obj, (row, col), (PATCH, PATCH))
            grad_obj = lax.dynamic_update_slice(grad_obj, old_g + gpatch, (row, col))
            old_i = lax.dynamic_slice(illum, (row, col), (PATCH, PATCH))
            illum = lax.dynamic_update_slice(illum, old_i + lit, (row, col))
            grad_probe = grad_probe + jnp.conj(window)[None] * chi
            pnorm = pnorm + alive * (window.real ** 2 + window.imag ** 2)
            return ((grad_obj, illum, grad_probe, pnorm), None)
        start = (jnp.zeros_like(dense), jnp.zeros_like(object_field[0]), jnp.zeros_like(modes), jnp.zeros_like(probe[0, 0]))
        (grad_obj, illum, grad_probe, pnorm), unused = lax.scan(visit, start, (amplitudes, positions, live))
        dense = dense - grad_obj / (illum + 1.0)
        modes = modes - grad_probe / (pnorm + 1.0)[None]
    new_object = jnp.stack([dense.real, dense.imag]).astype(object_field.dtype)
    new_probe = jnp.stack([modes.real, modes.imag]).astype(probe.dtype)
    return (new_object, new_probe)
```

```python
import functools

import jax
import jax.numpy as jnp
import ml_dtypes
import numpy as np
from jax import lax
from jax.experimental import pallas as pl
from jax.experimental.pallas import tpu as pltpu
from jax.sharding import PartitionSpec as P

ITERS = 2
SIGMA = 0.5
VMEM_LIMIT = 50 * 1024 * 1024


def split_np(w):
    hi = w.astype(ml_dtypes.bfloat16)
    lo = (w - hi.astype(np.float64)).astype(ml_dtypes.bfloat16)
    return hi, lo


def dft_blocks(length):
    index = np.arange(length)
    angle = 2.0 * np.pi * ((index[:, None] * index[None, :]) % length) / length
    c = np.cos(angle) / np.sqrt(length)
    s = np.sin(angle) / np.sqrt(length)
    minus = np.block([[c, -s], [s, c]])
    plus = np.block([[c, s], [-s, c]])
    return minus, plus


def split(x):
    hi = x.astype(jnp.bfloat16)
    lo = (x - hi.astype(jnp.float32)).astype(jnp.bfloat16)
    return hi, lo


def dot(a, b):
    return lax.dot_general(a, b, (((1,), (0,)), ((), ())), preferred_element_type=jnp.float32)


def right_product(x, w_ref):
    hi, lo = split(x)
    return dot(jnp.concatenate([hi, lo, hi], axis=1), w_ref[...])


def left_product(w_ref, x):
    hi, lo = split(x)
    return dot(w_ref[...], jnp.concatenate([hi, hi, lo], axis=0))


def pattern_kernel(
    rows_ref, cols_ref, count_ref, own_ref, below_ref, probe_ref, amp_ref,
    rf_ref, rb_ref, lf_ref, lb_ref,
    gown_ref, gover_ref, terms_ref,
    frame, grad,
):
    strip = own_ref.shape[1]
    columns = own_ref.shape[2]
    nmodes, length = probe_ref.shape[1], probe_ref.shape[2]
    for t in range(columns // 128):
        frame[:, t, :strip, :] = own_ref[:, :, t * 128 : (t + 1) * 128]
        frame[:, t, strip:, :] = below_ref[:, :, t * 128 : (t + 1) * 128]
    grad[...] = jnp.zeros_like(grad)
    terms_ref[...] = jnp.zeros_like(terms_ref)
    count = count_ref[0]

    def one(slot):
        alive = (slot < count).astype(jnp.float32)
        row = rows_ref[slot]
        col = cols_ref[slot]
        tile = jnp.minimum(col // 128, columns // 128 - 2)
        shift = col - tile * 128
        back = lax.rem(256 - shift, 256)

        def cut(part):
            wide = jnp.concatenate([frame[part, tile + k, pl.ds(row, length), :] for k in range(2)], axis=1)
            return pltpu.roll(wide, back, 1)[:, :length]

        xr, xi = cut(0), cut(1)
        waves = []
        for m in range(nmodes):
            pr, pi = probe_ref[0, m], probe_ref[1, m]
            waves.append(jnp.concatenate([pr * xr - pi * xi, pr * xi + pi * xr], axis=1))
        mids = [right_product(w, rf_ref) for w in waves]
        cols_in = jnp.concatenate(
            [jnp.concatenate([y[:, :length], y[:, length:]], axis=0) for y in mids], axis=1
        )
        far = left_product(lf_ref, cols_in)
        sq = far * far
        power = sq[:length] + sq[length:]
        intensity = functools.reduce(
            lambda a, b: a + b, [power[:, m * length : (m + 1) * length] for m in range(nmodes)]
        )
        weight = (1.0 - amp_ref[slot] * lax.rsqrt(intensity + SIGMA)) * alive
        weight = jnp.concatenate([weight] * nmodes, axis=1)
        weight = jnp.concatenate([weight, weight], axis=0)
        back_mid = left_product(lb_ref, far * weight)
        gr = gi = None
        for m in range(nmodes):
            piece = back_mid[:, m * length : (m + 1) * length]
            chi = right_product(jnp.concatenate([piece[:length], piece[length:]], axis=1), rb_ref)
            cr, ci = chi[:, :length], chi[:, length:]
            pr, pi = probe_ref[0, m], probe_ref[1, m]
            a = pr * cr + pi * ci
            b = pr * ci - pi * cr
            gr = a if gr is None else gr + a
            gi = b if gi is None else gi + b
            terms_ref[m] += xr * cr + xi * ci
            terms_ref[nmodes + m] += xr * ci - xi * cr
        terms_ref[2 * nmodes] += (xr * xr + xi * xi) * alive
        pad = jnp.zeros_like(gr)
        for part, g in enumerate((gr, gi)):
            wide = pltpu.roll(jnp.concatenate([g, pad], axis=1), shift, 1)
            for k in range(2):
                grad[part, tile + k, pl.ds(row, length), :] += wide[:, k * 128 : (k + 1) * 128]

    def step(index, carry):
        one(index)
        return carry

    lax.fori_loop(0, count, step, 0)
    for t in range(columns // 128):
        gown_ref[:, :, t * 128 : (t + 1) * 128] = grad[:, t, :strip, :]
        gover_ref[:, :, t * 128 : (t + 1) * 128] = grad[:, t, strip:, :]


def vmem():
    return pl.BlockSpec(memory_space=pltpu.VMEM)


def smem():
    return pl.BlockSpec(memory_space=pltpu.SMEM)


def patterns(rows, cols, count, own, below, probe, amps):
    length, nmodes = probe.shape[-1], probe.shape[1]
    strip, columns = own.shape[1:]
    minus, plus = dft_blocks(length)
    mh, ml = split_np(minus)
    ph, plo = split_np(plus)
    rf = np.concatenate([mh, mh, ml], axis=0)
    rb = np.concatenate([ph, ph, plo], axis=0)
    lf = np.concatenate([ph, plo, ph], axis=1)
    lb = np.concatenate([mh, ml, mh], axis=1)
    slots = amps.shape[0]
    macs = slots * nmodes * 4 * length * 3 * 4 * length * length
    return pl.pallas_call(
        pattern_kernel,
        out_shape=(
            jax.ShapeDtypeStruct((2, strip, columns), jnp.float32),
            jax.ShapeDtypeStruct((2, strip, columns), jnp.float32),
            jax.ShapeDtypeStruct((2 * nmodes + 1, length, length), jnp.float32),
        ),
        in_specs=[smem()] * 3 + [vmem()] * 8,
        out_specs=(vmem(), vmem(), vmem()),
        scratch_shapes=[
            pltpu.VMEM((2, columns // 128, 2 * strip, 128), jnp.float32),
            pltpu.VMEM((2, columns // 128, 2 * strip, 128), jnp.float32),
        ],
        compiler_params=pltpu.CompilerParams(vmem_limit_bytes=VMEM_LIMIT),
        cost_estimate=pl.CostEstimate(flops=2 * macs, bytes_accessed=8 * 1024 * 1024, transcendentals=0),
        name="patterns",
    )(rows, cols, count, own, below, probe, amps, *map(jnp.asarray, (rf, rb, lf, lb)))


def light_kernel(nsets, strip, scal_ref, probe_ref, out_ref, acc):
    nmodes, length = probe_ref.shape[1], probe_ref.shape[2]
    tiles = acc.shape[0]
    acc[...] = jnp.zeros_like(acc)
    power = None
    for m in range(nmodes):
        term = probe_ref[0, m] * probe_ref[0, m] + probe_ref[1, m] * probe_ref[1, m]
        power = term if power is None else power + term
    wide0 = jnp.concatenate([power, jnp.zeros_like(power)], axis=1)
    for s in range(nsets):

        def step(slot, carry, s=s):
            row = scal_ref[s, slot] + s * strip
            col = scal_ref[s, 16 + slot]
            tile = jnp.minimum(col // 128, tiles - 2)
            wide = pltpu.roll(wide0, col - tile * 128, 1)
            for k in range(2):
                acc[tile + k, pl.ds(row, length), :] += wide[:, k * 128 : (k + 1) * 128]
            return carry

        lax.fori_loop(0, scal_ref[s, 32], step, 0)
    for s in range(nsets - 1):
        for t in range(tiles):
            out_ref[s, :, t * 128 : (t + 1) * 128] = acc[t, (s + 1) * strip : (s + 2) * strip, :]


def light(scalars, probe, strip, columns):
    nsets = scalars.shape[0]
    return pl.pallas_call(
        functools.partial(light_kernel, nsets, strip),
        out_shape=jax.ShapeDtypeStruct((nsets - 1, strip, columns), jnp.float32),
        in_specs=[smem(), vmem()],
        out_specs=vmem(),
        scratch_shapes=[pltpu.VMEM((columns // 128, (nsets + 1) * strip, 128), jnp.float32)],
        compiler_params=pltpu.CompilerParams(vmem_limit_bytes=VMEM_LIMIT),
        cost_estimate=pl.CostEstimate(flops=16 * nsets * 40000, bytes_accessed=4 * 1024 * 1024, transcendentals=0),
        name="light",
    )(scalars, probe)


def shift_by(value, steps):
    count = lax.axis_size("dev")
    return lax.ppermute(
        value, "dev", [(i, i + steps) for i in range(count) if 0 <= i + steps < count]
    )


def rotate(value, stride, extent, steps):
    count = lax.axis_size("dev")

    def target(i):
        z = (i // stride) % extent
        return i + ((z + steps) % extent - z) * stride

    return lax.ppermute(value, "dev", [(i, target(i)) for i in range(count)])


def ring_scatter(value, stride, extent):
    place = (lax.axis_index("dev") // stride) % extent
    total = lax.dynamic_index_in_dim(value, place, 0, keepdims=False)
    for k in range(1, extent):
        piece = lax.dynamic_index_in_dim(value, lax.rem(place + k, extent), 0, keepdims=False)
        total = total + rotate(piece, stride, extent, k)
    return total


def ring_sum(value, stride, extent):
    total = value
    for k in range(1, extent):
        total = total + rotate(value, stride, extent, k)
    return total


def ring_gather(value, stride, extent):
    place = (lax.axis_index("dev") // stride) % extent
    out = jnp.zeros((extent,) + value.shape, value.dtype)
    out = lax.dynamic_update_index_in_dim(out, value, place, 0)
    for k in range(1, extent):
        got = rotate(value, stride, extent, k)
        out = lax.dynamic_update_index_in_dim(out, got, lax.rem(place + extent - k, extent), 0)
    return out


def sum_all(terms):
    shape = terms.shape
    flat = terms.reshape(2, -1, 128)
    flat = ring_scatter(flat, 1, 2)
    flat = ring_scatter(flat.reshape(4, -1, 128), 2, 4)
    flat = ring_sum(flat, 8, 4)
    flat = ring_sum(flat, 32, 4)
    flat = ring_gather(flat, 2, 4).reshape(-1, 128)
    return ring_gather(flat, 1, 2).reshape(shape)


def shards(object_field, probe, amplitudes, positions, counts):
    strip, columns = object_field.shape[1:]
    nmodes, length = probe.shape[1], probe.shape[-1]
    device = lax.axis_index("dev")
    rows = positions[:, 0] - device * strip
    cols = positions[:, 1]
    mine = jnp.concatenate([rows, cols, counts])
    current = object_field
    below = shift_by(current, -1)
    prev = shift_by(mine, 1)
    following = shift_by(mine, -1)
    lit = light(jnp.stack([prev, mine, following]), probe, strip, columns)

    def new_probe(terms):
        summed = sum_all(terms)
        grad = summed[: 2 * nmodes].reshape(2, nmodes, length, length)
        return probe - grad / (summed[2 * nmodes] + 1.0)[None, None]

    gown, gover, terms = patterns(rows, cols, counts, current, below, probe, amplitudes)
    from_above = shift_by(gover, 1)
    from_below = shift_by(gown, -1)
    probe = new_probe(terms)
    current = current - (gown + from_above) / (lit[0] + 1.0)[None]
    below = below - (gover + from_below) / (lit[1] + 1.0)[None]

    gown, gover, terms = patterns(rows, cols, counts, current, below, probe, amplitudes)
    from_above = shift_by(gover, 1)
    lit = light(jnp.stack([prev, mine]), probe, strip, columns)
    probe = new_probe(terms)
    current = current - (gown + from_above) / (lit[0] + 1.0)[None]
    return (current, probe)


def solution(mesh):
    placed = (P(None, "dev", None), P(), P("dev", None, None), P("dev", None), P("dev"))
    return jax.shard_map(
        shards, mesh=mesh, in_specs=placed, out_specs=(P(None, "dev", None), P()), check_vma=False
    )
```

```python
import functools

import jax
import jax.numpy as jnp
import ml_dtypes
import numpy as np
from jax import lax
from jax.experimental import pallas as pl
from jax.experimental.pallas import tpu as pltpu
from jax.sharding import PartitionSpec as P

SIGMA = 0.5
NSLOT, OFF_SLOT, OFF_PAIR = 2, 1, 0
STEP_TILES = 4
VMEM_LIMIT = 56 * 1024 * 1024


def split_np(w):
    hi = w.astype(ml_dtypes.bfloat16)
    lo = (w - hi.astype(np.float64)).astype(ml_dtypes.bfloat16)
    return hi, lo


def dft_blocks(length):
    index = np.arange(length)
    angle = 2.0 * np.pi * ((index[:, None] * index[None, :]) % length) / length
    c = np.cos(angle) / np.sqrt(length)
    s = np.sin(angle) / np.sqrt(length)
    minus = np.block([[c, -s], [s, c]])
    plus = np.block([[c, s], [-s, c]])
    return minus, plus


def split(x):
    hi = x.astype(jnp.bfloat16)
    lo = (x - hi.astype(jnp.float32)).astype(jnp.bfloat16)
    return hi, lo


def dot(a, b):
    return lax.dot_general(a, b, (((1,), (0,)), ((), ())), preferred_element_type=jnp.float32)


def right_product(x, w_ref):
    hi, lo = split(x)
    return dot(jnp.concatenate([hi, lo, hi], axis=1), w_ref[...])


def left_product(w_ref, x):
    n = x.shape[0]
    hi, lo = split(x)
    both = dot(w_ref[...], hi)
    return both[:n] + both[n:] + dot(w_ref[:n], lo)


def load_columns(ref, frame, rows, sems):
    return [
        pltpu.make_async_copy(ref.at[:, :, pl.ds(t * 128, 128)], frame.at[:, t, pl.ds(rows[0], rows[1] - rows[0]), :], sems.at[t])
        for t in range(frame.shape[1])
    ]


def start_all(copies):
    for copy in copies:
        copy.start()


def wait_all(copies):
    for copy in copies:
        copy.wait()


def pattern_kernel(stage, scal_ref, *refs):
    refs = list(refs)
    take = lambda n: [refs.pop(0) for _ in range(n)]
    objects = take({"own": 2, "above": 2, "both": 4}[stage])
    before = take(2) if stage == "above" else None
    amps = take(2 if stage == "both" else 1)
    whole = take(5)
    outs = take({"own": 2, "above": 4, "both": 6}[stage])
    frame, grad, terms_ref, amp_ref, probe_ref, rf_ref, rb_ref, lf_ref, lb_ref, order, in_sems, tile_sems, out_sems = take(13)
    tiles, strip = frame.shape[1], frame.shape[2] // 2
    quarter = strip // 2
    nmodes, length = probe_ref.shape[1], probe_ref.shape[2]
    slots = amp_ref.shape[0] // len(amps)
    width = 2 * slots + 2
    owners = {"own": (0,), "above": (1,), "both": (0, 1)}[stage]

    moves = list(zip(whole, (probe_ref, rf_ref, rb_ref, lf_ref, lb_ref)))
    moves += [(ref, amp_ref.at[pl.ds(k * slots, slots)]) for k, ref in enumerate(amps)]
    if stage == "both":
        share, extra = take(2)
        moves += [(objects[0], frame), (objects[1], share)]
        moves += [(objects[2 + k], extra.at[:, :, pl.ds(k * strip, strip)]) for k in range(2)]
        copies = []
    elif stage == "own":
        copies = load_columns(objects[0], frame, (quarter, 3 * quarter), tile_sems.at[0])
        copies += load_columns(objects[1], frame, (3 * quarter, 4 * quarter), tile_sems.at[1])
    else:
        copies = load_columns(objects[0], frame, (0, quarter), tile_sems.at[0])
        copies += load_columns(objects[1], frame, (quarter, 3 * quarter), tile_sems.at[1])
        moves += [(before[0], grad.at[:, :, pl.ds(quarter, 3 * quarter)]), (before[1], terms_ref)]
    copies += [pltpu.make_async_copy(src, dst, in_sems.at[k]) for k, (src, dst) in enumerate(moves)]
    start_all(copies)
    if stage == "above":
        grad[:, :, :quarter] = jnp.zeros((2, tiles, quarter, 128), jnp.float32)
    else:
        grad[...] = jnp.zeros_like(grad)
        terms_ref[...] = jnp.zeros_like(terms_ref)
    chosen = jnp.int32(0)
    for k, owner in enumerate(owners):
        for local in range(slots):
            order[chosen] = k * slots + local
            low = scal_ref[owner * width + local] >= quarter
            inside = (local < scal_ref[owner * width + 2 * slots]) & (low if owner else jnp.logical_not(low))
            chosen = chosen + inside.astype(jnp.int32)
    wait_all(copies)
    late = []
    if stage == "both":

        def add_share(t, carry):
            for part in range(2):
                frame[part, t] -= extra[part, t] * share[t]
            return carry

        lax.fori_loop(0, tiles, add_share, 0)
        late.append(pltpu.make_async_copy(frame.at[:, :, pl.ds(quarter, strip)], outs[5], out_sems.at[5]))
        start_all(late)
    h = length // 2
    pairs = nmodes // 2

    def place(slot):
        owner = slot // slots if len(owners) > 1 else owners[0]
        at = owner * width + slot % slots
        col = scal_ref[at + slots]
        tile = jnp.minimum(col // 128, tiles - 2)
        return scal_ref[at] + quarter - owner * strip, tile, col - tile * 128

    def stream(slot, shared, p):
        row, tile, shift = shared["place"]
        if p == 0:
            back = lax.rem(256 - shift, 256)

            def cut(part):
                wide = jnp.concatenate([frame[part, tile + k, pl.ds(row, length), :] for k in range(2)], axis=1)
                return pltpu.roll(wide, back, 1)[:, :length]

            shared["x"] = (cut(0), cut(1))
        xr, xi = shared["x"]
        modes = (2 * p, 2 * p + 1)
        waves = []
        for m in modes:
            pr, pi = probe_ref[0, m], probe_ref[1, m]
            waves.append(split(jnp.concatenate([pr * xr - pi * xi, pr * xi + pi * xr], axis=1)))
        yield
        mids = [dot(jnp.concatenate([hi, lo, hi], axis=1), rf_ref[...]) for hi, lo in waves]
        yield
        top = jnp.concatenate([jnp.concatenate([y[:h, :length] for y in mids], axis=1), jnp.concatenate([y[:h, length:] for y in mids], axis=1)], axis=0)
        low = jnp.concatenate([jnp.concatenate([y[h:, :length] for y in mids], axis=1), jnp.concatenate([y[h:, length:] for y in mids], axis=1)], axis=0)
        sums = [jnp.concatenate(split(v), axis=0) for v in (top + low, top - low)]
        yield
        fars = [dot(lf_ref[k], v) for k, v in enumerate(sums)]
        yield
        fars = [f[:length] + f[length:] for f in fars]
        sq = [f * f for f in fars]
        sq = [q[:h] + q[h:] for q in sq]
        shared.setdefault("power", []).extend(q[:, k * length : (k + 1) * length] for k in range(2) for q in [jnp.concatenate(sq, axis=0)])
        yield
        while len(shared["power"]) < nmodes:
            yield
        if "weight" not in shared:
            intensity = functools.reduce(lambda a, b: a + b, shared["power"])
            amp = jnp.concatenate([amp_ref[slot, pl.ds(k, h, stride=2), :] for k in range(2)], axis=0)
            shared["weight"] = (1.0 - amp * lax.rsqrt(intensity + SIGMA)) * shared["alive"]
        w = jnp.concatenate([shared["weight"]] * 2, axis=1)
        ins = [split(f * jnp.concatenate([wk, wk], axis=0)) for f, wk in zip(fars, (w[:h], w[h:]))]
        yield
        u, v = [dot(lb_ref[k], jnp.concatenate(x, axis=0)) for k, x in enumerate(ins)]
        yield
        u, v = u[:length] + u[length:], v[:length] + v[length:]
        a, b = u + v, u - v
        ins = []
        for k in range(2):
            c = slice(k * length, (k + 1) * length)
            re = jnp.concatenate([a[:h, c], b[:h, c]], axis=0)
            im = jnp.concatenate([a[h:, c], b[h:, c]], axis=0)
            ins.append(split(jnp.concatenate([re, im], axis=1)))
        yield
        chis = [dot(jnp.concatenate([hi, lo, hi], axis=1), rb_ref[...]) for hi, lo in ins]
        yield
        for m, chi in zip(modes, chis):
            cr, ci = chi[:, :length], chi[:, length:]
            pr, pi = probe_ref[0, m], probe_ref[1, m]
            a = pr * cr + pi * ci
            b = pr * ci - pi * cr
            g = shared.get("g")
            shared["g"] = (a, b) if g is None else (g[0] + a, g[1] + b)
            terms_ref[m * length : (m + 1) * length] += xr * cr + xi * ci
            terms_ref[(nmodes + m) * length : (nmodes + m + 1) * length] += xr * ci - xi * cr
        shared["done"] = shared.get("done", 0) + 1
        if shared["done"] == pairs:
            terms_ref[2 * nmodes * length :] += (xr * xr + xi * xi) * shared["alive"]
            pad = jnp.zeros((length, 128), jnp.float32)
            for part, g in enumerate(shared["g"]):
                wide = pltpu.roll(jnp.concatenate([g, pad], axis=1), shift, 1)
                for k in range(2):
                    grad[part, tile + k, pl.ds(row, length), :] += wide[:, k * 128 : (k + 1) * 128]
        yield

    def step(index, carry):
        streams = []
        for k in range(NSLOT):
            slot = order[jnp.minimum(NSLOT * index + k, jnp.maximum(chosen - 1, 0))]
            shared = {"place": place(slot), "alive": (NSLOT * index + k < chosen).astype(jnp.float32)}
            for p in range(pairs):
                streams.append([OFF_SLOT * k + OFF_PAIR * p, stream(slot, shared, p)])
        tick = 0
        while streams:
            for entry in list(streams):
                if tick >= entry[0]:
                    try:
                        next(entry[1])
                    except StopIteration:
                        streams.remove(entry)
            tick += 1
        return carry

    lax.fori_loop(0, (chosen + NSLOT - 1) // NSLOT, step, 0)
    if stage == "own":
        moves = [(grad.at[:, :, pl.ds(quarter, 3 * quarter)], outs[0]), (terms_ref, outs[1])]
    else:
        if stage == "above":
            moves = [(grad.at[:, :, pl.ds(k * strip, strip)], outs[k]) for k in range(2)]
        else:
            cuts = ((0, quarter), (3 * quarter, quarter), (quarter, strip))
            moves = [(grad.at[:, :, pl.ds(first, rows)], out) for (first, rows), out in zip(cuts, outs)]
        half = terms_ref.shape[0] // 2
        core = scal_ref[2 * slots + 1]
        k = len(moves)
        moves.append((terms_ref.at[pl.ds(pl.multiple_of(core * half, 8), half)], outs[k]))
        moves.append((terms_ref.at[pl.ds(pl.multiple_of((1 - core) * half, 8), half)], outs[k + 1]))
    copies = [pltpu.make_async_copy(src, dst, out_sems.at[k]) for k, (src, dst) in enumerate(moves)]
    start_all(copies)
    wait_all(copies + late)


def half_product(w_ref, which, x):
    n = x.shape[0]
    hi, lo = split(x)
    both = dot(w_ref[which], jnp.concatenate([hi, lo], axis=0))
    return both[:n] + both[n:]


def half_blocks(length):
    n = np.arange(length // 2)
    forward, backward = [], []
    for parity in range(2):
        angle = 2.0 * np.pi * (((2 * n[:, None] + parity) * n[None, :]) % length) / length
        c, s = np.cos(angle) / np.sqrt(length), np.sin(angle) / np.sqrt(length)
        forward.append(np.block([[c, s], [-s, c]]))
        backward.append(np.block([[c.T, -s.T], [s.T, c.T]]))
    out = []
    for mats in (forward, backward):
        both = []
        for w in mats:
            hi, lo = split_np(w)
            both.append(np.block([[hi, hi], [lo, lo]]))
        out.append(np.stack(both))
    return out


def vmem():
    return pl.BlockSpec(memory_space=pltpu.VMEM)


def smem():
    return pl.BlockSpec(memory_space=pltpu.SMEM)


def anywhere():
    return pl.BlockSpec(memory_space=pl.ANY)


def f32(*shape):
    return jax.ShapeDtypeStruct(shape, jnp.float32)


def patterns(stage, scalars, objects, before, amps, probe, tiles, flops):
    length, nmodes = probe.shape[-1], probe.shape[1]
    slots = amps[0].shape[0]
    strip = length
    minus, plus = dft_blocks(length)
    mh, ml = split_np(minus)
    ph, plo = split_np(plus)
    mats = (np.concatenate([mh, mh, ml], axis=0), np.concatenate([ph, ph, plo], axis=0)) + tuple(half_blocks(length))
    rows = (2 * nmodes + 1) * length
    half = f32(rows // 2, length)
    frame = (2, tiles, 2 * strip, 128)
    grads = [f32(2, tiles, n, 128) for n in (strip // 2, strip, 3 * strip // 2)]
    out_shape = {
        "own": (grads[2], f32(rows, length)),
        "above": (grads[1], grads[1], half, half),
        "both": (grads[0], grads[0], grads[1], half, half, grads[1]),
    }[stage]
    arrays = list(objects) + list(before or ()) + list(amps) + [probe]
    out_specs = tuple(vmem() if shape is half else anywhere() for shape in out_shape)
    return pl.pallas_call(
        functools.partial(pattern_kernel, stage),
        out_shape=out_shape,
        in_specs=[smem()] + [anywhere()] * (len(arrays) + len(mats)),
        out_specs=out_specs,
        scratch_shapes=[
            pltpu.VMEM(frame, jnp.float32),
            pltpu.VMEM(frame, jnp.float32),
            pltpu.VMEM((rows, length), jnp.float32),
            pltpu.VMEM((len(amps) * slots,) + amps[0].shape[1:], jnp.float32),
            pltpu.VMEM(probe.shape, jnp.float32),
        ]
        + [pltpu.VMEM(m.shape, jnp.bfloat16) for m in mats]
        + [
            pltpu.SMEM((2 * slots + 1,), jnp.int32),
            pltpu.SemaphoreType.DMA((11,)),
            pltpu.SemaphoreType.DMA((2, tiles)),
            pltpu.SemaphoreType.DMA((6,)),
        ]
        + ([pltpu.VMEM(frame[1:], jnp.float32), pltpu.VMEM(frame, jnp.float32)] if stage == "both" else []),
        compiler_params=pltpu.CompilerParams(vmem_limit_bytes=VMEM_LIMIT),
        cost_estimate=pl.CostEstimate(flops=flops, bytes_accessed=1024, transcendentals=0),
        name="patterns_" + stage,
    )(scalars, *arrays, *map(jnp.asarray, mats))


def light_kernel(nsets, strip, first, natural, scal_ref, probe_hbm, *refs):
    objects, grads = refs[: 3 if natural else 1], refs[3 if natural else 1 : 5 if natural else 2]
    pre_ref, share_ref, acc, frame, grad, probe_ref, tile_sems, sems = refs[len(objects) + len(grads) :]
    tiles = acc.shape[0]
    rows = frame.shape[2]
    length, nmodes = probe_ref.shape[2], probe_ref.shape[1]
    if natural:
        half = strip // 2
        spans = ((0, half), (half, 3 * half), (3 * half, 4 * half))
        copies = [c for k, (ref, span) in enumerate(zip(objects, spans)) for c in load_columns(ref, frame, span, tile_sems.at[k])]
        moves = [(ref, grad.at[:, :, pl.ds(k * strip, strip)]) for k, ref in enumerate(grads)]
    else:
        copies = []
        moves = [(objects[0], frame), (grads[0], grad)]
    load = pltpu.make_async_copy(probe_hbm, probe_ref, sems.at[0])
    copies += [pltpu.make_async_copy(src, dst, sems.at[1 + k]) for k, (src, dst) in enumerate(moves)]
    start_all([load] + copies)
    acc[...] = jnp.zeros_like(acc)
    load.wait()
    power = None
    for m in range(nmodes):
        term = probe_ref[0, m] * probe_ref[0, m] + probe_ref[1, m] * probe_ref[1, m]
        power = term if power is None else power + term
    wide0 = jnp.concatenate([power, jnp.zeros_like(power)], axis=1)
    width = scal_ref.shape[0] // nsets
    for s in range(nsets):

        def step(slot, carry, s=s):
            row = scal_ref[s * width + slot] + s * strip
            col = scal_ref[s * width + 16 + slot]
            tile = jnp.minimum(col // 128, tiles - 2)
            wide = pltpu.roll(wide0, col - tile * 128, 1)
            for k in range(2):
                acc[tile + k, pl.ds(row, length), :] += wide[:, k * 128 : (k + 1) * 128]
            return carry

        lax.fori_loop(0, scal_ref[s * width + 32], step, 0)
    wait_all(copies)

    def combine(t, carry):
        share = 1.0 / (acc[t, first : first + rows] + 1.0)
        acc[t, first : first + rows] = share
        for part in range(2):
            frame[part, t] -= grad[part, t] * share
        return carry

    lax.fori_loop(0, tiles, combine, 0)
    stores = [
        pltpu.make_async_copy(frame, pre_ref, sems.at[3]),
        pltpu.make_async_copy(acc.at[:, pl.ds(first, rows)], share_ref, sems.at[4]),
    ]
    start_all(stores)
    wait_all(stores)


def light(scalars, probe, objects, grads, nsets, strip, tiles, first, rows):
    natural = len(objects) == 3
    return pl.pallas_call(
        functools.partial(light_kernel, nsets, strip, first, natural),
        out_shape=(f32(2, tiles, rows, 128), f32(tiles, rows, 128)),
        in_specs=[smem()] + [anywhere()] * (1 + len(objects) + len(grads)),
        out_specs=(anywhere(), anywhere()),
        scratch_shapes=[
            pltpu.VMEM((tiles, (nsets + 1) * strip, 128), jnp.float32),
            pltpu.VMEM((2, tiles, rows, 128), jnp.float32),
            pltpu.VMEM((2, tiles, rows, 128), jnp.float32),
            pltpu.VMEM(probe.shape, jnp.float32),
            pltpu.SemaphoreType.DMA((3, tiles)),
            pltpu.SemaphoreType.DMA((5,)),
        ],
        compiler_params=pltpu.CompilerParams(vmem_limit_bytes=VMEM_LIMIT),
        cost_estimate=pl.CostEstimate(flops=16 * nsets * 40000, bytes_accessed=16 * 1024 * 1024, transcendentals=0),
        name="light",
    )(scalars, probe, *objects, *grads)


def last_kernel(pre, share, above_in, below_in, out):
    half = above_in.shape[2]
    for t in range(pre.shape[1]):
        c = slice(t * 128, (t + 1) * 128)
        for part in range(2):
            for k, got in enumerate((above_in, below_in)):
                r = slice(k * half, (k + 1) * half)
                out[part, r, c] = pre[part, t, r] - got[part, t] * share[t, r]


def last(pre, share, above_in, below_in):
    tiles, strip = pre.shape[1:3]

    def block(rows):
        return pl.BlockSpec((2, STEP_TILES, rows, 128), lambda j: (0, j, 0, 0))

    return pl.pallas_call(
        last_kernel,
        out_shape=f32(2, strip, tiles * 128),
        grid=(tiles // STEP_TILES,),
        in_specs=[block(strip), pl.BlockSpec((STEP_TILES, strip, 128), lambda j: (j, 0, 0)), block(strip // 2), block(strip // 2)],
        out_specs=pl.BlockSpec((2, strip, STEP_TILES * 128), lambda j: (0, 0, j)),
        compiler_params=pltpu.CompilerParams(vmem_limit_bytes=VMEM_LIMIT),
        cost_estimate=pl.CostEstimate(flops=4 * strip * tiles * 128, bytes_accessed=7 * 1024 * 1024, transcendentals=0),
        name="last",
    )(pre, share, above_in, below_in)


def shift_by(value, steps):
    count = lax.axis_size("dev")
    return lax.ppermute(
        value, "dev", [(i, i + steps) for i in range(count) if 0 <= i + steps < count]
    )


def rotate(value, stride, extent, steps):
    count = lax.axis_size("dev")

    def target(i):
        z = (i // stride) % extent
        return i + ((z + steps) % extent - z) * stride

    return lax.ppermute(value, "dev", [(i, target(i)) for i in range(count)])


def ring_scatter(value, stride, extent):
    place = (lax.axis_index("dev") // stride) % extent
    total = lax.dynamic_index_in_dim(value, place, 0, keepdims=False)
    for k in range(1, extent):
        piece = lax.dynamic_index_in_dim(value, lax.rem(place + k, extent), 0, keepdims=False)
        total = total + rotate(piece, stride, extent, k)
    return total


def ring_sum(value, stride, extent):
    total = value
    for k in range(1, extent):
        total = total + rotate(value, stride, extent, k)
    return total


def ring_gather(value, stride, extent):
    place = (lax.axis_index("dev") // stride) % extent
    out = jnp.zeros((extent,) + value.shape, value.dtype)
    out = lax.dynamic_update_index_in_dim(out, value, place, 0)
    for k in range(1, extent):
        got = rotate(value, stride, extent, k)
        out = lax.dynamic_update_index_in_dim(out, got, lax.rem(place + extent - k, extent), 0)
    return out


def sum_parts(keep, send):
    part = keep + rotate(send, 1, 2, 1)
    part = ring_scatter(part.reshape(4, -1, 128), 32, 4)
    part = ring_sum(part, 8, 4)
    return ring_sum(part, 2, 4)


def shards(object_field, probe, amplitudes, positions, counts):
    strip, columns = object_field.shape[1:]
    nmodes, length = probe.shape[1], probe.shape[-1]
    half, tiles = strip // 2, columns // 128
    barrier = lax.optimization_barrier
    device = lax.axis_index("dev")
    mine = jnp.concatenate([positions[:, 0] - device * strip, positions[:, 1], counts, (device % 2)[None]])

    def moved(probe, part):
        summed = ring_gather(part, 1, 2).reshape(2 * nmodes + 1, length, length)
        grad = summed[: 2 * nmodes].reshape(2, nmodes, length, length)
        return probe - grad / (summed[2 * nmodes] + 1.0)[None, None]

    def reduced(keep, send):
        part = sum_parts(keep, send)
        return ring_gather(part, 32, 4).reshape(-1, 128)

    below = shift_by(object_field[:, :half], -1)
    prev = shift_by(mine, 1)
    second = shift_by(mine, 2)
    following = shift_by(mine, -1)
    above = shift_by(object_field[:, half:], 1)
    amps = (amplitudes, shift_by(amplitudes, 1))
    before = patterns("own", mine, (object_field, below), None, amps[:1], probe, tiles, 1000)
    prev, second, following, above, got, before = barrier((prev, second, following, above, amps[1], before))
    amps = (amplitudes, got)
    scalars = jnp.concatenate([mine, prev])
    gtop, gbot, keep, send = patterns("above", scalars, (above, object_field), before, amps[1:], probe, tiles, 10**9)
    above_in = shift_by(gbot, 1)
    below_in = shift_by(gtop, -1)
    near = jnp.concatenate([second, prev, mine, following])
    pre, share = light(near, probe, (above, object_field, below), (gtop, gbot), 4, strip, tiles, strip + half, 2 * strip)
    above_in, below_in, pre, share, keep, send = barrier((above_in, below_in, pre, share, keep, send))
    probe = moved(probe, reduced(keep, send))

    gtop, gbot, gmid, keep, send, mid = patterns("both", scalars, (pre, share, above_in, below_in), None, amps, probe, tiles, 10**9)
    above_in = shift_by(gbot, 1)
    below_in = shift_by(gtop, -1)
    pre, share = light(jnp.concatenate([prev, mine]), probe, (mid,), (gmid,), 2, strip, tiles, strip, strip)
    above_in, below_in, pre, share, keep, send = barrier((above_in, below_in, pre, share, keep, send))
    part = sum_parts(keep, send)
    current = last(pre, share, above_in, below_in)
    part = ring_gather(part, 32, 4).reshape(-1, 128)
    current, part = barrier((current, part))
    return (current, moved(probe, part))


def solution(mesh):
    placed = (P(None, "dev", None), P(), P("dev", None, None), P("dev", None), P("dev"))
    return jax.shard_map(
        shards, mesh=mesh, in_specs=placed, out_specs=(P(None, "dev", None), P()), check_vma=False
    )
```

```python
import functools

import jax
import jax.numpy as jnp
import ml_dtypes
import numpy as np
from jax import lax
from jax.experimental import pallas as pl
from jax.experimental.pallas import tpu as pltpu
from jax.sharding import PartitionSpec as P

SIGMA = 0.5
NSLOT, OFF_SLOT, OFF_PAIR = 2, 1, 0
STEP_TILES = 4
MIB = 1024 * 1024
PATTERN_LIMITS = {"own": 20 * MIB, "above": 24 * MIB, "both": 30 * MIB}
VMEM_LIMIT = 20 * MIB


def split_np(w):
    hi = w.astype(ml_dtypes.bfloat16)
    lo = (w - hi.astype(np.float64)).astype(ml_dtypes.bfloat16)
    return hi, lo


def dft_blocks(length):
    index = np.arange(length)
    angle = 2.0 * np.pi * ((index[:, None] * index[None, :]) % length) / length
    c = np.cos(angle) / np.sqrt(length)
    s = np.sin(angle) / np.sqrt(length)
    minus = np.block([[c, -s], [s, c]])
    plus = np.block([[c, s], [-s, c]])
    return minus, plus


def split(x):
    hi = x.astype(jnp.bfloat16)
    lo = (x - hi.astype(jnp.float32)).astype(jnp.bfloat16)
    return hi, lo


def dot(a, b):
    return lax.dot_general(a, b, (((1,), (0,)), ((), ())), preferred_element_type=jnp.float32)


def right_product(x, w_ref):
    hi, lo = split(x)
    return dot(jnp.concatenate([hi, lo, hi], axis=1), w_ref[...])


def left_product(w_ref, x):
    n = x.shape[0]
    hi, lo = split(x)
    both = dot(w_ref[...], hi)
    return both[:n] + both[n:] + dot(w_ref[:n], lo)


def load_columns(ref, frame, rows, sems):
    return [
        pltpu.make_async_copy(ref.at[:, pl.ds(0, rows[1] - rows[0]), pl.ds(t * 128, 128)], frame.at[:, t, pl.ds(rows[0], rows[1] - rows[0]), :], sems.at[t])
        for t in range(frame.shape[1])
    ]


def start_all(copies):
    for copy in copies:
        copy.start()


def wait_all(copies):
    for copy in copies:
        copy.wait()


def pattern_kernel(stage, *refs):
    refs = list(refs)
    take = lambda n: [refs.pop(0) for _ in range(n)]
    scals = take(1 if stage == "own" else 2)
    objects = take({"own": 2, "above": 2, "both": 1}[stage])
    before = take(2) if stage == "above" else None
    amps = take(2 if stage == "both" else 1)
    whole = take(2)
    outs = take({"own": 2, "above": 4, "both": 5}[stage])
    frame, grad, terms_ref, order, tile_sems, out_sems = take(6)
    mats_ref = take(1)[0]
    moves = [(whole[1], mats_ref)]
    if stage == "own":
        grad, terms_ref = outs
        moves += list(zip(whole[:1] + amps, refs))
        whole, amps = refs[:1], refs[1:]
    probe_ref = whole[0]
    size = mats_ref.shape[1]
    rf_ref, rb_ref = (mats_ref.at[pl.ds(3 * size * k, 3 * size)] for k in range(2))
    lf_ref, lb_ref = ([mats_ref.at[pl.ds(size * (6 + 2 * k + n), size)] for n in range(2)] for k in range(2))
    tiles, strip = frame.shape[1], frame.shape[2] // 2
    quarter = strip // 2
    nmodes, length = probe_ref.shape[1], probe_ref.shape[2]
    slots = amps[0].shape[0]
    owners = {"own": (0,), "above": (1,), "both": (0, 1)}[stage]

    copies = []
    if stage == "own":
        copies = load_columns(objects[0], frame, (quarter, 3 * quarter), tile_sems.at[0])
        copies += load_columns(objects[1], frame, (3 * quarter, 4 * quarter), tile_sems.at[1])
    elif stage == "above":
        copies = load_columns(objects[0], frame, (0, quarter), tile_sems.at[0])
        copies += load_columns(objects[1], frame, (quarter, 3 * quarter), tile_sems.at[1])
    else:
        copies = [pltpu.make_async_copy(objects[0], frame, tile_sems.at[0, 0])]
    copies += [pltpu.make_async_copy(src, dst, out_sems.at[k]) for k, (src, dst) in enumerate(moves)]
    start_all(copies)
    if stage == "above":

        def take_over(t, carry):
            grad[:, t] = before[0][:, t]
            return carry

        lax.fori_loop(0, tiles, take_over, 0)
        terms_ref[...] = before[1][...]
    else:
        grad[...] = jnp.zeros_like(grad)
        terms_ref[...] = jnp.zeros_like(terms_ref)
    chosen = jnp.int32(0)
    for k, owner in enumerate(owners):
        for local in range(slots):
            order[chosen] = k * slots + local
            low = scals[owner][local] >= quarter
            inside = (local < scals[owner][2 * slots]) & (low if owner else jnp.logical_not(low))
            chosen = chosen + inside.astype(jnp.int32)
    wait_all(copies)
    def amplitude(slot, k, h):
        if len(amps) == 1:
            return amps[0][slot, pl.ds(k, h, stride=2), :]
        local = slot % slots
        return jnp.where(slot < slots, amps[0][local, pl.ds(k, h, stride=2), :], amps[1][local, pl.ds(k, h, stride=2), :])

    h = length // 2
    pairs = nmodes // 2

    def place(slot):
        if len(owners) == 1:
            row, col = (scals[owners[0]][slot + k * slots] for k in range(2))
            row = row - owners[0] * strip
        else:
            local = slot % slots
            first = slot < slots
            row, col = (jnp.where(first, scals[0][local + k * slots], scals[1][local + k * slots]) for k in range(2))
            row = jnp.where(first, row, row - strip)
        tile = jnp.minimum(col // 128, tiles - 2)
        return row + quarter, tile, col - tile * 128

    def stream(slot, shared, p):
        row, tile, shift = shared["place"]
        if p == 0:
            back = lax.rem(256 - shift, 256)

            def cut(part):
                wide = jnp.concatenate([frame[part, tile + k, pl.ds(row, length), :] for k in range(2)], axis=1)
                return pltpu.roll(wide, back, 1)[:, :length]

            shared["x"] = (cut(0), cut(1))
        xr, xi = shared["x"]
        modes = (2 * p, 2 * p + 1)
        waves = []
        for m in modes:
            pr, pi = probe_ref[0, m], probe_ref[1, m]
            waves.append(split(jnp.concatenate([pr * xr - pi * xi, pr * xi + pi * xr], axis=1)))
        yield
        mids = [dot(jnp.concatenate([hi, lo, hi], axis=1), rf_ref[...]) for hi, lo in waves]
        yield
        top = jnp.concatenate([jnp.concatenate([y[:h, :length] for y in mids], axis=1), jnp.concatenate([y[:h, length:] for y in mids], axis=1)], axis=0)
        low = jnp.concatenate([jnp.concatenate([y[h:, :length] for y in mids], axis=1), jnp.concatenate([y[h:, length:] for y in mids], axis=1)], axis=0)
        sums = [jnp.concatenate(split(v), axis=0) for v in (top + low, top - low)]
        yield
        fars = [dot(lf_ref[k][...], v) for k, v in enumerate(sums)]
        yield
        fars = [f[:length] + f[length:] for f in fars]
        sq = [f * f for f in fars]
        sq = [q[:h] + q[h:] for q in sq]
        shared.setdefault("power", []).extend(q[:, k * length : (k + 1) * length] for k in range(2) for q in [jnp.concatenate(sq, axis=0)])
        yield
        while len(shared["power"]) < nmodes:
            yield
        if "weight" not in shared:
            intensity = functools.reduce(lambda a, b: a + b, shared["power"])
            amp = jnp.concatenate([amplitude(slot, k, h) for k in range(2)], axis=0)
            shared["weight"] = (1.0 - amp * lax.rsqrt(intensity + SIGMA)) * shared["alive"]
        w = jnp.concatenate([shared["weight"]] * 2, axis=1)
        ins = [split(f * jnp.concatenate([wk, wk], axis=0)) for f, wk in zip(fars, (w[:h], w[h:]))]
        yield
        u, v = [dot(lb_ref[k][...], jnp.concatenate(x, axis=0)) for k, x in enumerate(ins)]
        yield
        u, v = u[:length] + u[length:], v[:length] + v[length:]
        a, b = u + v, u - v
        ins = []
        for k in range(2):
            c = slice(k * length, (k + 1) * length)
            re = jnp.concatenate([a[:h, c], b[:h, c]], axis=0)
            im = jnp.concatenate([a[h:, c], b[h:, c]], axis=0)
            ins.append(split(jnp.concatenate([re, im], axis=1)))
        yield
        chis = [dot(jnp.concatenate([hi, lo, hi], axis=1), rb_ref[...]) for hi, lo in ins]
        yield
        for m, chi in zip(modes, chis):
            cr, ci = chi[:, :length], chi[:, length:]
            pr, pi = probe_ref[0, m], probe_ref[1, m]
            a = pr * cr + pi * ci
            b = pr * ci - pi * cr
            g = shared.get("g")
            shared["g"] = (a, b) if g is None else (g[0] + a, g[1] + b)
            terms_ref[m * length : (m + 1) * length] += xr * cr + xi * ci
            terms_ref[(nmodes + m) * length : (nmodes + m + 1) * length] += xr * ci - xi * cr
        shared["done"] = shared.get("done", 0) + 1
        if shared["done"] == pairs:
            terms_ref[2 * nmodes * length :] += (xr * xr + xi * xi) * shared["alive"]
            pad = jnp.zeros((length, 128), jnp.float32)
            for part, g in enumerate(shared["g"]):
                wide = pltpu.roll(jnp.concatenate([g, pad], axis=1), shift, 1)
                for k in range(2):
                    grad[part, tile + k, pl.ds(row, length), :] += wide[:, k * 128 : (k + 1) * 128]
        yield

    def step(index, carry):
        streams = []
        for k in range(NSLOT):
            slot = order[jnp.minimum(NSLOT * index + k, jnp.maximum(chosen - 1, 0))]
            shared = {"place": place(slot), "alive": (NSLOT * index + k < chosen).astype(jnp.float32)}
            for p in range(pairs):
                streams.append([OFF_SLOT * k + OFF_PAIR * p, stream(slot, shared, p)])
        tick = 0
        while streams:
            for entry in list(streams):
                if tick >= entry[0]:
                    try:
                        next(entry[1])
                    except StopIteration:
                        streams.remove(entry)
            tick += 1
        return carry

    lax.fori_loop(0, (chosen + NSLOT - 1) // NSLOT, step, 0)
    if stage == "own":
        return
    half = terms_ref.shape[0] // 2
    core = scals[0][2 * slots + 1]
    if stage == "above":
        moves = [(grad.at[:, :, pl.ds(k * strip, strip)], outs[k]) for k in range(2)]
    else:
        cuts = ((0, quarter), (3 * quarter, quarter), (quarter, strip))
        moves = [(grad.at[:, :, pl.ds(first, rows)], out) for (first, rows), out in zip(cuts, outs)]
    copies = [pltpu.make_async_copy(src, dst, out_sems.at[k]) for k, (src, dst) in enumerate(moves)]
    copies.append(pltpu.make_async_copy(terms_ref.at[pl.ds(pl.multiple_of((1 - core) * half, 8), half)], outs[-1], out_sems.at[5]))
    start_all(copies)
    outs[len(moves)][...] = terms_ref[pl.ds(pl.multiple_of(core * half, 8), half), :]
    wait_all(copies)


def half_product(w_ref, which, x):
    n = x.shape[0]
    hi, lo = split(x)
    both = dot(w_ref[which], jnp.concatenate([hi, lo], axis=0))
    return both[:n] + both[n:]


def half_blocks(length):
    n = np.arange(length // 2)
    forward, backward = [], []
    for parity in range(2):
        angle = 2.0 * np.pi * (((2 * n[:, None] + parity) * n[None, :]) % length) / length
        c, s = np.cos(angle) / np.sqrt(length), np.sin(angle) / np.sqrt(length)
        forward.append(np.block([[c, s], [-s, c]]))
        backward.append(np.block([[c.T, -s.T], [s.T, c.T]]))
    out = []
    for mats in (forward, backward):
        both = []
        for w in mats:
            hi, lo = split_np(w)
            both.append(np.block([[hi, hi], [lo, lo]]))
        out.append(np.stack(both))
    return out


def vmem():
    return pl.BlockSpec(memory_space=pltpu.VMEM)


def smem():
    return pl.BlockSpec(memory_space=pltpu.SMEM)


def hbm():
    return pl.BlockSpec(memory_space=pltpu.HBM)


def anywhere():
    return pl.BlockSpec(memory_space=pl.ANY)


def f32(*shape):
    return jax.ShapeDtypeStruct(shape, jnp.float32)


def patterns(stage, scalars, objects, before, amps, probe, tiles, flops):
    length, nmodes = probe.shape[-1], probe.shape[1]
    slots = amps[0].shape[0]
    strip = length
    minus, plus = dft_blocks(length)
    mh, ml = split_np(minus)
    ph, plo = split_np(plus)
    mats = np.concatenate([mh, mh, ml, ph, ph, plo] + [m.reshape(-1, 2 * length) for m in half_blocks(length)], axis=0)
    rows = (2 * nmodes + 1) * length
    half = f32(rows // 2, length)
    frame = (2, tiles, 2 * strip, 128)
    grads = [f32(2, tiles, n, 128) for n in (strip // 2, strip, 3 * strip // 2)]
    out_shape = {
        "own": (f32(*frame), f32(rows, length)),
        "above": (grads[1], grads[1], half, half),
        "both": (grads[0], grads[0], grads[1], half, half),
    }[stage]
    arrays = list(objects) + list(before or ()) + list(amps) + [probe]
    out_specs = tuple(vmem() if shape is half or stage == "own" else anywhere() for shape in out_shape)
    if stage != "own":
        out_specs = out_specs[:-1] + (hbm(),)
    kinds = [hbm() if stage == "both" else anywhere()] * len(objects)
    kinds += [anywhere() if stage == "own" else vmem()] * (len(arrays) - len(objects)) + [hbm()]
    small = [pltpu.VMEM((8, 128), jnp.float32)] * 2
    return pl.pallas_call(
        functools.partial(pattern_kernel, stage),
        out_shape=out_shape,
        in_specs=[smem()] * len(scalars) + kinds,
        out_specs=out_specs,
        scratch_shapes=[pltpu.VMEM(frame, jnp.float32)]
        + (small if stage == "own" else [pltpu.VMEM(frame, jnp.float32), pltpu.VMEM((rows, length), jnp.float32)])
        + [
            pltpu.SMEM((2 * slots + 1,), jnp.int32),
            pltpu.SemaphoreType.DMA((2, tiles)),
            pltpu.SemaphoreType.DMA((6,)),
        ]
        + [pltpu.VMEM(a.shape, a.dtype) for a in [mats] + ([probe] + list(amps) if stage == "own" else [])],
        compiler_params=pltpu.CompilerParams(vmem_limit_bytes=PATTERN_LIMITS[stage]),
        cost_estimate=pl.CostEstimate(flops=flops, bytes_accessed=1024, transcendentals=0),
        name="patterns_" + stage,
    )(*scalars, *arrays, jnp.asarray(mats))


def light_kernel(nsets, strip, first, natural, *refs):
    scals, probe_hbm, refs = refs[:nsets], refs[nsets], refs[nsets + 1 :]
    objects, grads = refs[: 3 if natural else 1], refs[3 if natural else 1 : 5 if natural else 2]
    pre_ref, share_ref, acc, frame, grad, probe_ref, tile_sems, sems = refs[len(objects) + len(grads) :]
    tiles = acc.shape[0]
    rows = frame.shape[2]
    length, nmodes = probe_ref.shape[2], probe_ref.shape[1]
    if natural:
        half = strip // 2
        spans = ((0, half), (half, 3 * half), (3 * half, 4 * half))
        copies = [c for k, (ref, span) in enumerate(zip(objects, spans)) for c in load_columns(ref, frame, span, tile_sems.at[k])]
        moves = [(ref, grad.at[:, :, pl.ds(k * strip, strip)]) for k, ref in enumerate(grads)]
    else:
        copies = []
        moves = [(objects[0].at[:, :, pl.ds(strip // 2, rows)], frame), (grads[0], grad)]
    load = pltpu.make_async_copy(probe_hbm, probe_ref, sems.at[0])
    copies += [pltpu.make_async_copy(src, dst, sems.at[1 + k]) for k, (src, dst) in enumerate(moves)]
    start_all([load] + copies)
    acc[...] = jnp.zeros_like(acc)
    load.wait()
    power = None
    for m in range(nmodes):
        term = probe_ref[0, m] * probe_ref[0, m] + probe_ref[1, m] * probe_ref[1, m]
        power = term if power is None else power + term
    wide0 = jnp.concatenate([power, jnp.zeros_like(power)], axis=1)
    for s in range(nsets):

        def step(slot, carry, s=s):
            row = scals[s][slot] + s * strip
            col = scals[s][16 + slot]
            tile = jnp.minimum(col // 128, tiles - 2)
            wide = pltpu.roll(wide0, col - tile * 128, 1)
            for k in range(2):
                acc[tile + k, pl.ds(row, length), :] += wide[:, k * 128 : (k + 1) * 128]
            return carry

        lax.fori_loop(0, scals[s][32], step, 0)
    wait_all(copies)

    def combine(t, carry):
        share = 1.0 / (acc[t, first : first + rows] + 1.0)
        acc[t, first : first + rows] = share
        for part in range(2):
            frame[part, t] -= grad[part, t] * share
        return carry

    lax.fori_loop(0, tiles, combine, 0)
    stores = [
        pltpu.make_async_copy(frame, pre_ref, sems.at[3]),
        pltpu.make_async_copy(acc.at[:, pl.ds(first, rows)], share_ref, sems.at[4]),
    ]
    start_all(stores)
    wait_all(stores)


def light(scalars, probe, objects, grads, strip, tiles, first, rows):
    natural = len(objects) == 3
    nsets = len(scalars)
    return pl.pallas_call(
        functools.partial(light_kernel, nsets, strip, first, natural),
        out_shape=(f32(2, tiles, rows, 128), f32(tiles, rows, 128)),
        in_specs=[smem()] * nsets + [anywhere()] * (1 + len(objects) + len(grads)),
        out_specs=(anywhere(), anywhere()),
        scratch_shapes=[
            pltpu.VMEM((tiles, (nsets + 1) * strip, 128), jnp.float32),
            pltpu.VMEM((2, tiles, rows, 128), jnp.float32),
            pltpu.VMEM((2, tiles, rows, 128), jnp.float32),
            pltpu.VMEM(probe.shape, jnp.float32),
            pltpu.SemaphoreType.DMA((3, tiles)),
            pltpu.SemaphoreType.DMA((5,)),
        ],
        compiler_params=pltpu.CompilerParams(vmem_limit_bytes=VMEM_LIMIT),
        cost_estimate=pl.CostEstimate(flops=16 * nsets * 40000, bytes_accessed=16 * 1024 * 1024, transcendentals=0),
        name="light",
    )(*scalars, probe, *objects, *grads)


def meet_kernel(pre, share, above_in, below_in, out, frame, sems):
    strip = above_in.shape[2]

    def tile(t, carry):
        for part in range(2):
            for k, got in enumerate((above_in, below_in)):
                r = pl.ds(k * strip, strip)
                frame[part, t, r, :] = pre[part, t, r, :] - got[part, t] * share[t, r, :]
        pltpu.make_async_copy(frame.at[:, t], out.at[:, t], sems.at[t]).start()
        return carry

    lax.fori_loop(0, frame.shape[1], tile, 0)
    wait_all([pltpu.make_async_copy(frame.at[:, t], out.at[:, t], sems.at[t]) for t in range(frame.shape[1])])


def meet(pre, share, above_in, below_in):
    return pl.pallas_call(
        meet_kernel,
        out_shape=f32(*pre.shape),
        in_specs=[vmem()] * 4,
        out_specs=hbm(),
        scratch_shapes=[pltpu.VMEM(pre.shape, jnp.float32), pltpu.SemaphoreType.DMA((pre.shape[1],))],
        compiler_params=pltpu.CompilerParams(vmem_limit_bytes=VMEM_LIMIT),
        cost_estimate=pl.CostEstimate(flops=1000, bytes_accessed=16 * 1024 * 1024, transcendentals=0),
        name="meet",
    )(pre, share, above_in, below_in)


def last_kernel(pre, share, above_in, below_in, out):
    half = above_in.shape[2]
    for t in range(pre.shape[1]):
        c = slice(t * 128, (t + 1) * 128)
        for part in range(2):
            for k, got in enumerate((above_in, below_in)):
                r = slice(k * half, (k + 1) * half)
                out[part, r, c] = pre[part, t, r] - got[part, t] * share[t, r]


def last(pre, share, above_in, below_in):
    tiles, strip = pre.shape[1:3]

    def block(rows):
        return pl.BlockSpec((2, STEP_TILES, rows, 128), lambda j: (0, j, 0, 0))

    return pl.pallas_call(
        last_kernel,
        out_shape=f32(2, strip, tiles * 128),
        grid=(tiles // STEP_TILES,),
        in_specs=[block(strip), pl.BlockSpec((STEP_TILES, strip, 128), lambda j: (j, 0, 0)), block(strip // 2), block(strip // 2)],
        out_specs=pl.BlockSpec((2, strip, STEP_TILES * 128), lambda j: (0, 0, j)),
        compiler_params=pltpu.CompilerParams(vmem_limit_bytes=VMEM_LIMIT),
        cost_estimate=pl.CostEstimate(flops=4 * strip * tiles * 128, bytes_accessed=7 * 1024 * 1024, transcendentals=0),
        name="last",
    )(pre, share, above_in, below_in)


def shift_by(value, steps):
    count = lax.axis_size("dev")
    return lax.ppermute(
        value, "dev", [(i, i + steps) for i in range(count) if 0 <= i + steps < count]
    )


def rotate(value, stride, extent, steps):
    count = lax.axis_size("dev")

    def target(i):
        z = (i // stride) % extent
        return i + ((z + steps) % extent - z) * stride

    return lax.ppermute(value, "dev", [(i, target(i)) for i in range(count)])


def small_call(kernel, out_shape, operands, scratch=()):
    several = isinstance(out_shape, tuple)
    return pl.pallas_call(
        kernel,
        out_shape=out_shape,
        in_specs=[smem()] + [vmem()] * (len(operands) - 1),
        out_specs=(vmem(),) * len(out_shape) if several else vmem(),
        scratch_shapes=list(scratch),
        compiler_params=pltpu.CompilerParams(vmem_limit_bytes=8 * MIB),
        cost_estimate=pl.CostEstimate(flops=1000, bytes_accessed=1000, transcendentals=0),
        name=kernel.__name__,
    )(*operands)


PLACE = 34


def deal_kernel(scal_ref, keep, got, *outs):
    rows = outs[0].shape[0]
    for k, out in enumerate(outs):
        r = pl.ds(pl.multiple_of(lax.rem(scal_ref[PLACE] + k, len(outs)) * rows, 8), rows)
        out[...] = keep[r, :] + got[r, :]


def gather_kernel(scal_ref, *refs):
    pieces, out = refs[:-1], refs[-1]
    rows, count = pieces[0].shape[0], len(pieces)
    for k, piece in enumerate(pieces):
        r = pl.ds(pl.multiple_of(lax.rem(scal_ref[PLACE] + count - k, count) * rows, 8), rows)
        out[r, :] = piece[...]


def probe_kernel(scal_ref, mine, other, probe, out, summed):
    half = mine.shape[0]
    core = scal_ref[PLACE - 1]
    summed[pl.ds(pl.multiple_of(core * half, 8), half), :] = mine[...]
    summed[pl.ds(pl.multiple_of((1 - core) * half, 8), half), :] = other[...]
    parts, nmodes, length = probe.shape[:3]
    share = 1.0 / (summed[parts * nmodes * length :, :] + 1.0)
    for part in range(parts):
        for m in range(nmodes):
            first = (part * nmodes + m) * length
            out[part, m] = probe[part, m] - summed[first : first + length, :] * share


def ring_sum(own, pieces, stride):
    total = own
    for k, piece in enumerate(pieces):
        total = total + rotate(piece, stride, 4, k + 1)
    return total


def shards(object_field, probe, amplitudes, positions, counts):
    strip, columns = object_field.shape[1:]
    nmodes, length = probe.shape[1], probe.shape[-1]
    half, tiles = strip // 2, columns // 128
    barrier = lax.optimization_barrier
    device = lax.axis_index("dev")
    mine = jnp.concatenate([positions[:, 0] - device * strip, positions[:, 1], counts, (device % 2)[None], (device // 32 % 4)[None]])

    def scattered(keep, send):
        pieces = small_call(deal_kernel, (f32(keep.shape[0] // 4, length),) * 4, (mine, keep, rotate(send, 1, 2, 1)))
        return ring_sum(pieces[0], pieces[1:], 32)

    def gathered(part):
        for stride in (8, 2):
            part = ring_sum(part, (part,) * 3, stride)
        pieces = [part] + [rotate(part, 32, 4, k) for k in (1, 2, 3)]
        return small_call(gather_kernel, f32(4 * part.shape[0], length), [mine] + pieces)

    def moved(probe, half):
        terms = pltpu.VMEM((2 * half.shape[0], length), jnp.float32)
        return small_call(probe_kernel, f32(*probe.shape), (mine, half, rotate(half, 1, 2, 1), probe), (terms,))

    extra = jnp.pad(mine.astype(jnp.float32)[None, None], ((0, 1), (0, 7), (0, columns - mine.shape[0])))
    below = shift_by(jnp.concatenate([object_field[:, :half], extra], axis=1), -1)
    above = shift_by(jnp.concatenate([object_field[:, half:], extra], axis=1), 1)
    second = shift_by(mine, 2)
    amps = (amplitudes, shift_by(amplitudes, 1))
    before = patterns("own", (mine,), (object_field, below), None, amps[:1], probe, tiles, 1000)
    second, above, got, before = barrier((second, above, amps[1], before))
    amps = (amplitudes, got)
    prev, following = (a[0, half, : mine.shape[0]].astype(jnp.int32) for a in (above, below))
    scalars = (mine, prev)
    gtop, gbot, keep, send = patterns("above", scalars, (above, object_field), before, amps[1:], probe, tiles, 10**9)
    above_in = shift_by(gbot, 1)
    below_in = shift_by(gtop, -1)
    near = (second, prev, mine, following)
    pre, share = light(near, probe, (above, object_field, below), (gtop, gbot), strip, tiles, strip + half, 2 * strip)
    above_in, below_in, pre, share, part = barrier((above_in, below_in, pre, share, scattered(keep, send)))
    frame, part = barrier((meet(pre, share, above_in, below_in), part))
    probe = moved(probe, gathered(part))

    gtop, gbot, gmid, keep, send = patterns("both", scalars, (frame,), None, amps, probe, tiles, 10**9)
    above_in = shift_by(gbot, 1)
    below_in = shift_by(gtop, -1)
    pre, share = light((prev, mine), probe, (frame,), (gmid,), strip, tiles, strip, strip)
    above_in, below_in, pre, share, part = barrier((above_in, below_in, pre, share, scattered(keep, send)))
    current, part = barrier((last(pre, share, above_in, below_in), part))
    return (current, moved(probe, gathered(part)))


def solution(mesh):
    placed = (P(None, "dev", None), P(), P("dev", None, None), P("dev", None), P("dev"))
    return jax.shard_map(
        shards, mesh=mesh, in_specs=placed, out_specs=(P(None, "dev", None), P()), check_vma=False
    )
```

```python
import functools

import jax
import jax.numpy as jnp
import ml_dtypes
import numpy as np
from jax import lax
from jax.experimental import pallas as pl
from jax.experimental.pallas import tpu as pltpu
from jax.sharding import PartitionSpec as P

SIGMA = 0.5
NSLOT, OFF_SLOT, OFF_PAIR = 2, 1, 0
STEP_TILES = 4
MIB = 1024 * 1024
PATTERN_LIMITS = {"first": 20 * MIB, "second": 24 * MIB, "both": 30 * MIB}
PLACE = 34
VMEM_LIMIT = 20 * MIB


def split_np(w):
    hi = w.astype(ml_dtypes.bfloat16)
    lo = (w - hi.astype(np.float64)).astype(ml_dtypes.bfloat16)
    return hi, lo


def dft_blocks(length):
    index = np.arange(length)
    angle = 2.0 * np.pi * ((index[:, None] * index[None, :]) % length) / length
    c = np.cos(angle) / np.sqrt(length)
    s = np.sin(angle) / np.sqrt(length)
    minus = np.block([[c, -s], [s, c]])
    plus = np.block([[c, s], [-s, c]])
    return minus, plus


def split(x):
    hi = x.astype(jnp.bfloat16)
    lo = (x - hi.astype(jnp.float32)).astype(jnp.bfloat16)
    return hi, lo


def dot(a, b):
    return lax.dot_general(a, b, (((1,), (0,)), ((), ())), preferred_element_type=jnp.float32)


def right_product(x, w_ref):
    hi, lo = split(x)
    return dot(jnp.concatenate([hi, lo, hi], axis=1), w_ref[...])


def left_product(w_ref, x):
    n = x.shape[0]
    hi, lo = split(x)
    both = dot(w_ref[...], hi)
    return both[:n] + both[n:] + dot(w_ref[:n], lo)


def load_columns(ref, frame, first, rows, sems):
    return [
        pltpu.make_async_copy(ref.at[:, pl.ds(0, rows), pl.ds(t * 128, 128)], frame.at[:, t, pl.ds(first, rows), :], sems.at[t])
        for t in range(frame.shape[1])
    ]


def start_all(copies):
    for copy in copies:
        copy.start()


def wait_all(copies):
    for copy in copies:
        copy.wait()


def pattern_kernel(stage, *refs):
    refs = list(refs)
    take = lambda n: [refs.pop(0) for _ in range(n)]
    scals = take(2)
    objects = take({"first": 2, "second": 2, "both": 1}[stage])
    before = take(2) if stage == "second" else None
    amps = take(3 if stage == "both" else 2)
    probe_hbm, mats_hbm = take(2)
    outs = take({"first": 2, "second": 4, "both": 5}[stage])
    frame, grad, terms_ref, order, tile_sems, out_sems, mats_ref = take(7)
    core = scals[0][PLACE - 1]
    slots = amps[0].shape[0]
    moves = [(mats_hbm, mats_ref)]
    probe_ref = probe_hbm
    if stage == "first":
        grad, terms_ref = outs
        probe_ref, amp_ref = take(2)
        moves.append((probe_hbm, probe_ref))
    size = mats_ref.shape[1]
    rf_ref, rb_ref = (mats_ref.at[pl.ds(3 * size * k, 3 * size)] for k in range(2))
    lf_ref, lb_ref = ([mats_ref.at[pl.ds(size * (6 + 2 * k + n), size)] for n in range(2)] for k in range(2))
    tiles, strip = frame.shape[1], frame.shape[2] // 2
    quarter = strip // 2
    nmodes, length = probe_ref.shape[1], probe_ref.shape[2]

    if stage == "both":
        copies = [pltpu.make_async_copy(objects[0], frame, tile_sems.at[0, 0])]
    else:
        where = ((1 - core) if stage == "first" else core) * (3 * quarter)
        copies = load_columns(objects[0], frame, pl.multiple_of(where, 8), quarter, tile_sems.at[0])
        copies += load_columns(objects[1], frame, quarter, strip, tile_sems.at[1])
    copies += [pltpu.make_async_copy(src, dst, out_sems.at[k]) for k, (src, dst) in enumerate(moves)]
    start_all(copies)
    if stage == "first":
        choice = [pltpu.make_async_copy(amp, amp_ref, out_sems.at[5]) for amp in amps]
        for k in range(2):
            pl.when(core == k)(choice[k].start)
        copies.append(choice[0])
    if stage == "second":

        def take_over(t, carry):
            grad[:, t] = before[0][:, t]
            return carry

        lax.fori_loop(0, tiles, take_over, 0)
        terms_ref[...] = before[1][...]
    else:
        grad[...] = jnp.zeros_like(grad)
        terms_ref[...] = jnp.zeros_like(terms_ref)
    owners = {"first": (core,), "second": (1 - core,), "both": (0, 1)}[stage]
    chosen = jnp.int32(0)
    for k, owner in enumerate(owners):
        scal = scals[k if stage == "both" else 1]
        for local in range(slots):
            order[chosen] = k * slots + local
            inside = (local < scal[2 * slots]) & ((scal[local] >= quarter).astype(jnp.int32) == owner)
            chosen = chosen + inside.astype(jnp.int32)
    wait_all(copies)

    def amplitude(slot, k, h):
        def part(ref, index):
            return ref[index, pl.ds(k, h, stride=2), :]

        if stage == "first":
            return part(amp_ref, slot)
        local = slot % slots
        if stage == "second":
            return jnp.where(core == 0, part(amps[1], local), part(amps[0], local))
        others = jnp.where(core == 0, part(amps[2], local), part(amps[1], local))
        return jnp.where(slot < slots, part(amps[0], local), others)

    h = length // 2
    pairs = nmodes // 2

    def place(slot):
        local = slot % slots
        if stage == "both":
            first = slot < slots
            row, col = (jnp.where(first, scals[0][local + k * slots], scals[1][local + k * slots]) for k in range(2))
            row = jnp.where(first, row, row - strip)
        else:
            row, col = (scals[1][local + k * slots] for k in range(2))
            row = row - owners[0] * strip
        tile = jnp.minimum(col // 128, tiles - 2)
        return row + quarter, tile, col - tile * 128

    def stream(slot, shared, p):
        row, tile, shift = shared["place"]
        if p == 0:
            back = lax.rem(256 - shift, 256)

            def cut(part):
                wide = jnp.concatenate([frame[part, tile + k, pl.ds(row, length), :] for k in range(2)], axis=1)
                return pltpu.roll(wide, back, 1)[:, :length]

            shared["x"] = (cut(0), cut(1))
        xr, xi = shared["x"]
        modes = (2 * p, 2 * p + 1)
        waves = []
        for m in modes:
            pr, pi = probe_ref[0, m], probe_ref[1, m]
            waves.append(split(jnp.concatenate([pr * xr - pi * xi, pr * xi + pi * xr], axis=1)))
        yield
        mids = [dot(jnp.concatenate([hi, lo, hi], axis=1), rf_ref[...]) for hi, lo in waves]
        yield
        top = jnp.concatenate([jnp.concatenate([y[:h, :length] for y in mids], axis=1), jnp.concatenate([y[:h, length:] for y in mids], axis=1)], axis=0)
        low = jnp.concatenate([jnp.concatenate([y[h:, :length] for y in mids], axis=1), jnp.concatenate([y[h:, length:] for y in mids], axis=1)], axis=0)
        sums = [jnp.concatenate(split(v), axis=0) for v in (top + low, top - low)]
        yield
        fars = [dot(lf_ref[k][...], v) for k, v in enumerate(sums)]
        yield
        fars = [f[:length] + f[length:] for f in fars]
        sq = [f * f for f in fars]
        sq = [q[:h] + q[h:] for q in sq]
        shared.setdefault("power", []).extend(q[:, k * length : (k + 1) * length] for k in range(2) for q in [jnp.concatenate(sq, axis=0)])
        yield
        while len(shared["power"]) < nmodes:
            yield
        if "weight" not in shared:
            intensity = functools.reduce(lambda a, b: a + b, shared["power"])
            amp = jnp.concatenate([amplitude(slot, k, h) for k in range(2)], axis=0)
            shared["weight"] = (1.0 - amp * lax.rsqrt(intensity + SIGMA)) * shared["alive"]
        w = jnp.concatenate([shared["weight"]] * 2, axis=1)
        ins = [split(f * jnp.concatenate([wk, wk], axis=0)) for f, wk in zip(fars, (w[:h], w[h:]))]
        yield
        u, v = [dot(lb_ref[k][...], jnp.concatenate(x, axis=0)) for k, x in enumerate(ins)]
        yield
        u, v = u[:length] + u[length:], v[:length] + v[length:]
        a, b = u + v, u - v
        ins = []
        for k in range(2):
            c = slice(k * length, (k + 1) * length)
            re = jnp.concatenate([a[:h, c], b[:h, c]], axis=0)
            im = jnp.concatenate([a[h:, c], b[h:, c]], axis=0)
            ins.append(split(jnp.concatenate([re, im], axis=1)))
        yield
        chis = [dot(jnp.concatenate([hi, lo, hi], axis=1), rb_ref[...]) for hi, lo in ins]
        yield
        for m, chi in zip(modes, chis):
            cr, ci = chi[:, :length], chi[:, length:]
            pr, pi = probe_ref[0, m], probe_ref[1, m]
            a = pr * cr + pi * ci
            b = pr * ci - pi * cr
            g = shared.get("g")
            shared["g"] = (a, b) if g is None else (g[0] + a, g[1] + b)
            terms_ref[m * length : (m + 1) * length] += xr * cr + xi * ci
            terms_ref[(nmodes + m) * length : (nmodes + m + 1) * length] += xr * ci - xi * cr
        shared["done"] = shared.get("done", 0) + 1
        if shared["done"] == pairs:
            terms_ref[2 * nmodes * length :] += (xr * xr + xi * xi) * shared["alive"]
            pad = jnp.zeros((length, 128), jnp.float32)
            for part, g in enumerate(shared["g"]):
                wide = pltpu.roll(jnp.concatenate([g, pad], axis=1), shift, 1)
                for k in range(2):
                    grad[part, tile + k, pl.ds(row, length), :] += wide[:, k * 128 : (k + 1) * 128]
        yield

    def step(index, carry):
        streams = []
        for k in range(NSLOT):
            slot = order[jnp.minimum(NSLOT * index + k, jnp.maximum(chosen - 1, 0))]
            shared = {"place": place(slot), "alive": (NSLOT * index + k < chosen).astype(jnp.float32)}
            for p in range(pairs):
                streams.append([OFF_SLOT * k + OFF_PAIR * p, stream(slot, shared, p)])
        tick = 0
        while streams:
            for entry in list(streams):
                if tick >= entry[0]:
                    try:
                        next(entry[1])
                    except StopIteration:
                        streams.remove(entry)
            tick += 1
        return carry

    lax.fori_loop(0, (chosen + NSLOT - 1) // NSLOT, step, 0)
    if stage == "first":
        return
    half = terms_ref.shape[0] // 2
    rows, step = (strip, strip) if stage == "second" else (quarter, 3 * quarter)
    moves = [(grad.at[:, :, pl.ds(pl.multiple_of(k * step, 8), rows)], out) for k, out in zip((core, 1 - core), outs)]
    if stage == "both":
        moves.append((grad.at[:, :, pl.ds(quarter, strip)], outs[2]))
    copies = [pltpu.make_async_copy(src, dst, out_sems.at[k]) for k, (src, dst) in enumerate(moves)]
    copies.append(pltpu.make_async_copy(terms_ref.at[pl.ds(pl.multiple_of((1 - core) * half, 8), half)], outs[-1], out_sems.at[5]))
    start_all(copies)
    outs[len(moves)][...] = terms_ref[pl.ds(pl.multiple_of(core * half, 8), half), :]
    wait_all(copies)


def half_product(w_ref, which, x):
    n = x.shape[0]
    hi, lo = split(x)
    both = dot(w_ref[which], jnp.concatenate([hi, lo], axis=0))
    return both[:n] + both[n:]


def half_blocks(length):
    n = np.arange(length // 2)
    forward, backward = [], []
    for parity in range(2):
        angle = 2.0 * np.pi * (((2 * n[:, None] + parity) * n[None, :]) % length) / length
        c, s = np.cos(angle) / np.sqrt(length), np.sin(angle) / np.sqrt(length)
        forward.append(np.block([[c, s], [-s, c]]))
        backward.append(np.block([[c.T, -s.T], [s.T, c.T]]))
    out = []
    for mats in (forward, backward):
        both = []
        for w in mats:
            hi, lo = split_np(w)
            both.append(np.block([[hi, hi], [lo, lo]]))
        out.append(np.stack(both))
    return out


def vmem():
    return pl.BlockSpec(memory_space=pltpu.VMEM)


def smem():
    return pl.BlockSpec(memory_space=pltpu.SMEM)


def hbm():
    return pl.BlockSpec(memory_space=pltpu.HBM)


def anywhere():
    return pl.BlockSpec(memory_space=pl.ANY)


def f32(*shape):
    return jax.ShapeDtypeStruct(shape, jnp.float32)


def patterns(stage, scalars, objects, before, amps, probe, tiles, flops):
    length, nmodes = probe.shape[-1], probe.shape[1]
    slots = amps[0].shape[0]
    strip = length
    minus, plus = dft_blocks(length)
    mh, ml = split_np(minus)
    ph, plo = split_np(plus)
    mats = np.concatenate([mh, mh, ml, ph, ph, plo] + [m.reshape(-1, 2 * length) for m in half_blocks(length)], axis=0)
    rows = (2 * nmodes + 1) * length
    half = f32(rows // 2, length)
    frame = (2, tiles, 2 * strip, 128)
    grads = [f32(2, tiles, n, 128) for n in (strip // 2, strip, 3 * strip // 2)]
    out_shape = {
        "first": (f32(*frame), f32(rows, length)),
        "second": (grads[1], grads[1], half, half),
        "both": (grads[0], grads[0], grads[1], half, half),
    }[stage]
    arrays = list(objects) + list(before or ()) + list(amps) + [probe]
    out_specs = tuple(vmem() if shape is half or stage == "first" else anywhere() for shape in out_shape)
    if stage != "first":
        out_specs = out_specs[:-1] + (hbm(),)
    kinds = [hbm() if stage == "both" else anywhere()] * len(objects)
    kinds += [anywhere() if stage == "first" else vmem()] * (len(arrays) - len(objects)) + [hbm()]
    small = [pltpu.VMEM((8, 128), jnp.float32)] * 2
    return pl.pallas_call(
        functools.partial(pattern_kernel, stage),
        out_shape=out_shape,
        in_specs=[smem()] * len(scalars) + kinds,
        out_specs=out_specs,
        scratch_shapes=[pltpu.VMEM(frame, jnp.float32)]
        + (small if stage == "first" else [pltpu.VMEM(frame, jnp.float32), pltpu.VMEM((rows, length), jnp.float32)])
        + [
            pltpu.SMEM((2 * slots + 1,), jnp.int32),
            pltpu.SemaphoreType.DMA((2, tiles)),
            pltpu.SemaphoreType.DMA((6,)),
        ]
        + [pltpu.VMEM(a.shape, a.dtype) for a in [mats] + ([probe, amps[0]] if stage == "first" else [])],
        compiler_params=pltpu.CompilerParams(vmem_limit_bytes=PATTERN_LIMITS[stage]),
        cost_estimate=pl.CostEstimate(flops=flops, bytes_accessed=1024, transcendentals=0),
        name="patterns_" + stage,
    )(*scalars, *arrays, jnp.asarray(mats))


def light_kernel(nsets, strip, first, natural, *refs):
    scals, probe_hbm, refs = refs[:nsets], refs[nsets], refs[nsets + 1 :]
    objects, grads = refs[: 3 if natural else 1], refs[3 if natural else 1 : 5 if natural else 2]
    pre_ref, share_ref, acc, frame, grad, probe_ref, tile_sems, sems = refs[len(objects) + len(grads) :]
    tiles = acc.shape[0]
    rows = frame.shape[2]
    length, nmodes = probe_ref.shape[2], probe_ref.shape[1]
    if natural:
        half = strip // 2
        core = scals[2][PLACE - 1]
        firsts = [pl.multiple_of(k * 3 * half, 8) for k in (core, 1 - core)]
        copies = [c for k in range(2) for c in load_columns(objects[k], frame, firsts[k], half, tile_sems.at[k])]
        copies += load_columns(objects[2], frame, half, strip, tile_sems.at[2])
        moves = [(ref, grad.at[:, :, pl.ds(pl.multiple_of(k * strip, 8), strip)]) for k, ref in zip((core, 1 - core), grads)]
    else:
        copies = []
        moves = [(objects[0].at[:, :, pl.ds(strip // 2, rows)], frame), (grads[0], grad)]
    load = pltpu.make_async_copy(probe_hbm, probe_ref, sems.at[0])
    copies += [pltpu.make_async_copy(src, dst, sems.at[1 + k]) for k, (src, dst) in enumerate(moves)]
    start_all([load] + copies)
    acc[...] = jnp.zeros_like(acc)
    load.wait()
    power = None
    for m in range(nmodes):
        term = probe_ref[0, m] * probe_ref[0, m] + probe_ref[1, m] * probe_ref[1, m]
        power = term if power is None else power + term
    wide0 = jnp.concatenate([power, jnp.zeros_like(power)], axis=1)
    for s in range(nsets):

        def step(slot, carry, s=s):
            row = scals[s][slot] + s * strip
            col = scals[s][16 + slot]
            tile = jnp.minimum(col // 128, tiles - 2)
            wide = pltpu.roll(wide0, col - tile * 128, 1)
            for k in range(2):
                acc[tile + k, pl.ds(row, length), :] += wide[:, k * 128 : (k + 1) * 128]
            return carry

        lax.fori_loop(0, scals[s][32], step, 0)
    wait_all(copies)

    def combine(t, carry):
        share = 1.0 / (acc[t, first : first + rows] + 1.0)
        acc[t, first : first + rows] = share
        for part in range(2):
            frame[part, t] -= grad[part, t] * share
        return carry

    lax.fori_loop(0, tiles, combine, 0)
    stores = [
        pltpu.make_async_copy(frame, pre_ref, sems.at[3]),
        pltpu.make_async_copy(acc.at[:, pl.ds(first, rows)], share_ref, sems.at[4]),
    ]
    start_all(stores)
    wait_all(stores)


def light(scalars, probe, objects, grads, strip, tiles, first, rows):
    natural = len(objects) == 3
    nsets = len(scalars)
    return pl.pallas_call(
        functools.partial(light_kernel, nsets, strip, first, natural),
        out_shape=(f32(2, tiles, rows, 128), f32(tiles, rows, 128)),
        in_specs=[smem()] * nsets + [anywhere()] * (1 + len(objects) + len(grads)),
        out_specs=(anywhere(), anywhere()),
        scratch_shapes=[
            pltpu.VMEM((tiles, (nsets + 1) * strip, 128), jnp.float32),
            pltpu.VMEM((2, tiles, rows, 128), jnp.float32),
            pltpu.VMEM((2, tiles, rows, 128), jnp.float32),
            pltpu.VMEM(probe.shape, jnp.float32),
            pltpu.SemaphoreType.DMA((3, tiles)),
            pltpu.SemaphoreType.DMA((5,)),
        ],
        compiler_params=pltpu.CompilerParams(vmem_limit_bytes=VMEM_LIMIT),
        cost_estimate=pl.CostEstimate(flops=16 * nsets * 40000, bytes_accessed=16 * 1024 * 1024, transcendentals=0),
        name="light",
    )(*scalars, probe, *objects, *grads)


def meet_kernel(scal_ref, pre, share, cross, chip, out, frame, sems):
    strip = cross.shape[2]
    core = scal_ref[PLACE - 1]

    def tile(t, carry):
        for part in range(2):
            for k, got in ((core, cross), (1 - core, chip)):
                r = pl.ds(pl.multiple_of(k * strip, 8), strip)
                frame[part, t, r, :] = pre[part, t, r, :] - got[part, t] * share[t, r, :]
        pltpu.make_async_copy(frame.at[:, t], out.at[:, t], sems.at[t]).start()
        return carry

    lax.fori_loop(0, frame.shape[1], tile, 0)
    wait_all([pltpu.make_async_copy(frame.at[:, t], out.at[:, t], sems.at[t]) for t in range(frame.shape[1])])


def meet(scalars, pre, share, cross, chip):
    return pl.pallas_call(
        meet_kernel,
        out_shape=f32(*pre.shape),
        in_specs=[smem()] + [vmem()] * 4,
        out_specs=hbm(),
        scratch_shapes=[pltpu.VMEM(pre.shape, jnp.float32), pltpu.SemaphoreType.DMA((pre.shape[1],))],
        compiler_params=pltpu.CompilerParams(vmem_limit_bytes=VMEM_LIMIT),
        cost_estimate=pl.CostEstimate(flops=1000, bytes_accessed=16 * 1024 * 1024, transcendentals=0),
        name="meet",
    )(scalars, pre, share, cross, chip)


def last_kernel(scal_ref, pre, share, cross, chip, out):
    half = cross.shape[2]
    core = scal_ref[PLACE - 1]
    for t in range(pre.shape[1]):
        c = slice(t * 128, (t + 1) * 128)
        for part in range(2):
            for k, got in ((core, cross), (1 - core, chip)):
                r = pl.ds(pl.multiple_of(k * half, 8), half)
                out[part, r, c] = pre[part, t, r, :] - got[part, t] * share[t, r, :]


def last(scalars, pre, share, cross, chip):
    tiles, strip = pre.shape[1:3]

    def block(rows):
        return pl.BlockSpec((2, STEP_TILES, rows, 128), lambda j: (0, j, 0, 0))

    return pl.pallas_call(
        last_kernel,
        out_shape=f32(2, strip, tiles * 128),
        grid=(tiles // STEP_TILES,),
        in_specs=[smem(), block(strip), pl.BlockSpec((STEP_TILES, strip, 128), lambda j: (j, 0, 0)), block(strip // 2), block(strip // 2)],
        out_specs=pl.BlockSpec((2, strip, STEP_TILES * 128), lambda j: (0, 0, j)),
        compiler_params=pltpu.CompilerParams(vmem_limit_bytes=VMEM_LIMIT),
        cost_estimate=pl.CostEstimate(flops=4 * strip * tiles * 128, bytes_accessed=7 * 1024 * 1024, transcendentals=0),
        name="last",
    )(scalars, pre, share, cross, chip)


def shift_by(value, steps):
    count = lax.axis_size("dev")
    return lax.ppermute(
        value, "dev", [(i, i + steps) for i in range(count) if 0 <= i + steps < count]
    )


def rotate(value, stride, extent, steps):
    count = lax.axis_size("dev")

    def target(i):
        z = (i // stride) % extent
        return i + ((z + steps) % extent - z) * stride

    return lax.ppermute(value, "dev", [(i, target(i)) for i in range(count)])


def small_call(kernel, out_shape, operands, scratch=()):
    several = isinstance(out_shape, tuple)
    return pl.pallas_call(
        kernel,
        out_shape=out_shape,
        in_specs=[smem()] + [vmem()] * (len(operands) - 1),
        out_specs=(vmem(),) * len(out_shape) if several else vmem(),
        scratch_shapes=list(scratch),
        compiler_params=pltpu.CompilerParams(vmem_limit_bytes=8 * MIB),
        cost_estimate=pl.CostEstimate(flops=1000, bytes_accessed=1000, transcendentals=0),
        name=kernel.__name__,
    )(*operands)


def deal_kernel(scal_ref, keep, got, *outs):
    rows = outs[0].shape[0]
    for k, out in enumerate(outs):
        r = pl.ds(pl.multiple_of(lax.rem(scal_ref[PLACE] + k, len(outs)) * rows, 8), rows)
        out[...] = keep[r, :] + got[r, :]


def gather_kernel(scal_ref, *refs):
    pieces, out = refs[:-1], refs[-1]
    rows, count = pieces[0].shape[0], len(pieces)
    for k, piece in enumerate(pieces):
        r = pl.ds(pl.multiple_of(lax.rem(scal_ref[PLACE] + count - k, count) * rows, 8), rows)
        out[r, :] = piece[...]


def probe_kernel(scal_ref, mine, other, probe, out, summed):
    half = mine.shape[0]
    core = scal_ref[PLACE - 1]
    summed[pl.ds(pl.multiple_of(core * half, 8), half), :] = mine[...]
    summed[pl.ds(pl.multiple_of((1 - core) * half, 8), half), :] = other[...]
    parts, nmodes, length = probe.shape[:3]
    share = 1.0 / (summed[parts * nmodes * length :, :] + 1.0)
    for part in range(parts):
        for m in range(nmodes):
            first = (part * nmodes + m) * length
            out[part, m] = probe[part, m] - summed[first : first + length, :] * share


def ring_sum(own, pieces, stride):
    total = own
    for k, piece in enumerate(pieces):
        total = total + rotate(piece, stride, 4, k + 1)
    return total


def shards(object_field, probe, amplitudes, positions, counts):
    strip, columns = object_field.shape[1:]
    nmodes, length = probe.shape[1], probe.shape[-1]
    half, tiles = strip // 2, columns // 128
    barrier = lax.optimization_barrier
    device = lax.axis_index("dev")
    mine = jnp.concatenate([positions[:, 0] - device * strip, positions[:, 1], counts, (device % 2)[None], (device // 32 % 4)[None]])

    def scattered(keep, send):
        pieces = small_call(deal_kernel, (f32(keep.shape[0] // 4, length),) * 4, (mine, keep, rotate(send, 1, 2, 1)))
        return ring_sum(pieces[0], pieces[1:], 32)

    def gathered(part):
        for stride in (8, 2):
            part = ring_sum(part, (part,) * 3, stride)
        pieces = [part] + [rotate(part, 32, 4, k) for k in (1, 2, 3)]
        return small_call(gather_kernel, f32(4 * part.shape[0], length), [mine] + pieces)

    def moved(probe, half):
        terms = pltpu.VMEM((2 * half.shape[0], length), jnp.float32)
        return small_call(probe_kernel, f32(*probe.shape), (mine, half, rotate(half, 1, 2, 1), probe), (terms,))

    core = device % 2
    count = lax.axis_size("dev")
    chip_down = [(i, i + 1) for i in range(0, count, 2)]
    cross_down = [(i, i + 1) for i in range(1, count - 1, 2)]

    def swap(value, pairs):
        return lax.ppermute(value, "dev", pairs + [(j, i) for i, j in pairs])

    def exchange(cross, chip):
        return swap(cross, cross_down), swap(chip, chip_down)

    extra = jnp.pad(mine.astype(jnp.float32)[None, None], ((0, 1), (0, 7), (0, columns - mine.shape[0])))

    def edge(which):
        return jnp.concatenate([lax.dynamic_slice_in_dim(object_field, which * half, half, 1), extra], axis=1)

    def info(halo):
        return halo[0, half, : mine.shape[0]].astype(jnp.int32)

    cross, chip = exchange(edge(core), edge(1 - core))
    amps_cross = lax.ppermute(amplitudes, "dev", cross_down)
    amps_chip = lax.ppermute(amplitudes, "dev", chip_down)
    second = shift_by(mine, 2)
    from_chip = info(chip)
    amps = (amplitudes, amps_chip)
    before = patterns("first", (mine, jnp.where(core == 0, mine, from_chip)), (chip, object_field), None, amps, probe, tiles, 1000)
    second, cross, amps_cross, before = barrier((second, cross, amps_cross, before))
    from_cross = info(cross)
    chosen = jnp.where(core == 0, from_cross, mine)
    amps = (amplitudes, amps_cross)
    out, inner, keep, send = patterns("second", (mine, chosen), (cross, object_field), before, amps, probe, tiles, 10**9)
    got, got_inner = exchange(out, inner)
    prev = jnp.where(core == 0, from_cross, from_chip)
    following = jnp.where(core == 0, from_chip, from_cross)
    near = (second, prev, mine, following)
    pre, share = light(near, probe, (cross, chip, object_field), (out, inner), strip, tiles, strip + half, 2 * strip)
    got, got_inner, pre, share, part = barrier((got, got_inner, pre, share, scattered(keep, send)))
    frame, part = barrier((meet(mine, pre, share, got, got_inner), part))
    probe = moved(probe, gathered(part))

    amps = (amplitudes, amps_chip, amps_cross)
    out, inner, gmid, keep, send = patterns("both", (mine, prev), (frame,), None, amps, probe, tiles, 10**9)
    got, got_inner = exchange(out, inner)
    pre, share = light((prev, mine), probe, (frame,), (gmid,), strip, tiles, strip, strip)
    got, got_inner, pre, share, part = barrier((got, got_inner, pre, share, scattered(keep, send)))
    current, part = barrier((last(mine, pre, share, got, got_inner), part))
    return (current, moved(probe, gathered(part)))


def solution(mesh):
    placed = (P(None, "dev", None), P(), P("dev", None, None), P("dev", None), P("dev"))
    return jax.shard_map(
        shards, mesh=mesh, in_specs=placed, out_specs=(P(None, "dev", None), P()), check_vma=False
    )
```

```python
import functools

import jax
import jax.numpy as jnp
import ml_dtypes
import numpy as np
from jax import lax
from jax.experimental import pallas as pl
from jax.experimental.pallas import tpu as pltpu
from jax.sharding import PartitionSpec as P

SIGMA = 0.5
NSLOT, OFF_SLOT, OFF_PAIR = 2, 1, 0
STEP_TILES = 4
MIB = 1024 * 1024
PATTERN_LIMITS = {"first": 20 * MIB, "second": 24 * MIB, "both": 30 * MIB}
PLACE = 34
VMEM_LIMIT = 20 * MIB


def split_np(w):
    hi = w.astype(ml_dtypes.bfloat16)
    lo = (w - hi.astype(np.float64)).astype(ml_dtypes.bfloat16)
    return hi, lo


def dft_blocks(length):
    index = np.arange(length)
    angle = 2.0 * np.pi * ((index[:, None] * index[None, :]) % length) / length
    c = np.cos(angle) / np.sqrt(length)
    s = np.sin(angle) / np.sqrt(length)
    minus = np.block([[c, -s], [s, c]])
    plus = np.block([[c, s], [-s, c]])
    return minus, plus


def split(x):
    hi = x.astype(jnp.bfloat16)
    lo = (x - hi.astype(jnp.float32)).astype(jnp.bfloat16)
    return hi, lo


def dot(a, b):
    return lax.dot_general(a, b, (((1,), (0,)), ((), ())), preferred_element_type=jnp.float32)


def right_product(x, w_ref):
    hi, lo = split(x)
    return dot(jnp.concatenate([hi, lo, hi], axis=1), w_ref[...])


def left_product(w_ref, x):
    n = x.shape[0]
    hi, lo = split(x)
    both = dot(w_ref[...], hi)
    return both[:n] + both[n:] + dot(w_ref[:n], lo)


def load_columns(ref, frame, first, rows, sems):
    return [
        pltpu.make_async_copy(ref.at[:, pl.ds(0, rows), pl.ds(t * 128, 128)], frame.at[:, t, pl.ds(first, rows), :], sems.at[t])
        for t in range(frame.shape[1])
    ]


def start_all(copies):
    for copy in copies:
        copy.start()


def wait_all(copies):
    for copy in copies:
        copy.wait()


def pattern_kernel(stage, *refs):
    refs = list(refs)
    take = lambda n: [refs.pop(0) for _ in range(n)]
    scals = take(2)
    objects = take({"first": 2, "second": 2, "both": 1}[stage])
    before = take(2) if stage == "second" else None
    amps = take(3 if stage == "both" else 2)
    probe_hbm, mats_hbm = take(2)
    outs = take({"first": 2, "second": 4, "both": 5}[stage])
    frame, grad, terms_ref, order, tile_sems, out_sems, mats_ref = take(7)
    core = scals[0][PLACE - 1]
    slots = amps[0].shape[0]
    moves = [(mats_hbm, mats_ref)]
    probe_ref = probe_hbm
    if stage == "first":
        grad, terms_ref = outs
        probe_ref, amp_ref = take(2)
        moves.append((probe_hbm, probe_ref))
    size = mats_ref.shape[1]
    rf_ref, rb_ref = (mats_ref.at[pl.ds(3 * size * k, 3 * size)] for k in range(2))
    lf_ref, lb_ref = ([mats_ref.at[pl.ds(size * (6 + 2 * k + n), size)] for n in range(2)] for k in range(2))
    tiles, strip = frame.shape[1], frame.shape[2] // 2
    quarter = strip // 2
    nmodes, length = probe_ref.shape[1], probe_ref.shape[2]

    if stage == "both":
        copies = [pltpu.make_async_copy(objects[0], frame, tile_sems.at[0, 0])]
    else:
        where = ((1 - core) if stage == "first" else core) * (3 * quarter)
        copies = load_columns(objects[0], frame, pl.multiple_of(where, 8), quarter, tile_sems.at[0])
        copies += load_columns(objects[1], frame, quarter, strip, tile_sems.at[1])
    copies += [pltpu.make_async_copy(src, dst, out_sems.at[k]) for k, (src, dst) in enumerate(moves)]
    start_all(copies)
    if stage == "first":
        choice = [pltpu.make_async_copy(amp, amp_ref, out_sems.at[5]) for amp in amps]
        for k in range(2):
            pl.when(core == k)(choice[k].start)
        copies.append(choice[0])
    if stage == "second":

        def take_over(t, carry):
            grad[:, t] = before[0][:, t]
            return carry

        lax.fori_loop(0, tiles, take_over, 0)
        terms_ref[...] = before[1][...]
    else:
        grad[...] = jnp.zeros_like(grad)
        terms_ref[...] = jnp.zeros_like(terms_ref)
    owners = {"first": (core,), "second": (1 - core,), "both": (0, 1)}[stage]
    chosen = jnp.int32(0)
    for k, owner in enumerate(owners):
        scal = scals[k if stage == "both" else 1]
        for local in range(slots):
            order[chosen] = k * slots + local
            inside = (local < scal[2 * slots]) & ((scal[local] >= quarter).astype(jnp.int32) == owner)
            chosen = chosen + inside.astype(jnp.int32)
    wait_all(copies)

    def amplitude(slot, k, h):
        def part(ref, index):
            return ref[index, pl.ds(k, h, stride=2), :]

        if stage == "first":
            return part(amp_ref, slot)
        local = slot % slots
        if stage == "second":
            return jnp.where(core == 0, part(amps[1], local), part(amps[0], local))
        others = jnp.where(core == 0, part(amps[2], local), part(amps[1], local))
        return jnp.where(slot < slots, part(amps[0], local), others)

    h = length // 2
    pairs = nmodes // 2

    def place(slot):
        local = slot % slots
        if stage == "both":
            first = slot < slots
            row, col = (jnp.where(first, scals[0][local + k * slots], scals[1][local + k * slots]) for k in range(2))
            row = jnp.where(first, row, row - strip)
        else:
            row, col = (scals[1][local + k * slots] for k in range(2))
            row = row - owners[0] * strip
        tile = jnp.minimum(col // 128, tiles - 2)
        return row + quarter, tile, col - tile * 128

    def stream(slot, shared, p):
        row, tile, shift = shared["place"]
        if p == 0:
            back = lax.rem(256 - shift, 256)

            def cut(part):
                wide = jnp.concatenate([frame[part, tile + k, pl.ds(row, length), :] for k in range(2)], axis=1)
                return pltpu.roll(wide, back, 1)[:, :length]

            shared["x"] = (cut(0), cut(1))
        xr, xi = shared["x"]
        modes = (2 * p, 2 * p + 1)
        waves = []
        for m in modes:
            pr, pi = probe_ref[0, m], probe_ref[1, m]
            waves.append(split(jnp.concatenate([pr * xr - pi * xi, pr * xi + pi * xr], axis=1)))
        yield
        mids = [dot(jnp.concatenate([hi, lo, hi], axis=1), rf_ref[...]) for hi, lo in waves]
        yield
        top = jnp.concatenate([jnp.concatenate([y[:h, :length] for y in mids], axis=1), jnp.concatenate([y[:h, length:] for y in mids], axis=1)], axis=0)
        low = jnp.concatenate([jnp.concatenate([y[h:, :length] for y in mids], axis=1), jnp.concatenate([y[h:, length:] for y in mids], axis=1)], axis=0)
        sums = [jnp.concatenate(split(v), axis=0) for v in (top + low, top - low)]
        yield
        fars = [dot(lf_ref[k][...], v) for k, v in enumerate(sums)]
        yield
        fars = [f[:length] + f[length:] for f in fars]
        sq = [f * f for f in fars]
        sq = [q[:h] + q[h:] for q in sq]
        shared.setdefault("power", []).extend(q[:, k * length : (k + 1) * length] for k in range(2) for q in [jnp.concatenate(sq, axis=0)])
        yield
        while len(shared["power"]) < nmodes:
            yield
        if "weight" not in shared:
            intensity = functools.reduce(lambda a, b: a + b, shared["power"])
            amp = jnp.concatenate([amplitude(slot, k, h) for k in range(2)], axis=0)
            shared["weight"] = (1.0 - amp * lax.rsqrt(intensity + SIGMA)) * shared["alive"]
        w = jnp.concatenate([shared["weight"]] * 2, axis=1)
        ins = [split(f * jnp.concatenate([wk, wk], axis=0)) for f, wk in zip(fars, (w[:h], w[h:]))]
        yield
        u, v = [dot(lb_ref[k][...], jnp.concatenate(x, axis=0)) for k, x in enumerate(ins)]
        yield
        u, v = u[:length] + u[length:], v[:length] + v[length:]
        a, b = u + v, u - v
        ins = []
        for k in range(2):
            c = slice(k * length, (k + 1) * length)
            re = jnp.concatenate([a[:h, c], b[:h, c]], axis=0)
            im = jnp.concatenate([a[h:, c], b[h:, c]], axis=0)
            ins.append(split(jnp.concatenate([re, im], axis=1)))
        yield
        chis = [dot(jnp.concatenate([hi, lo, hi], axis=1), rb_ref[...]) for hi, lo in ins]
        yield
        for m, chi in zip(modes, chis):
            cr, ci = chi[:, :length], chi[:, length:]
            pr, pi = probe_ref[0, m], probe_ref[1, m]
            a = pr * cr + pi * ci
            b = pr * ci - pi * cr
            g = shared.get("g")
            shared["g"] = (a, b) if g is None else (g[0] + a, g[1] + b)
            terms_ref[m * length : (m + 1) * length] += xr * cr + xi * ci
            terms_ref[(nmodes + m) * length : (nmodes + m + 1) * length] += xr * ci - xi * cr
        shared["done"] = shared.get("done", 0) + 1
        if shared["done"] == pairs:
            terms_ref[2 * nmodes * length :] += (xr * xr + xi * xi) * shared["alive"]
            pad = jnp.zeros((length, 128), jnp.float32)
            for part, g in enumerate(shared["g"]):
                wide = pltpu.roll(jnp.concatenate([g, pad], axis=1), shift, 1)
                for k in range(2):
                    grad[part, tile + k, pl.ds(row, length), :] += wide[:, k * 128 : (k + 1) * 128]
        yield

    def step(index, carry):
        streams = []
        for k in range(NSLOT):
            slot = order[jnp.minimum(NSLOT * index + k, jnp.maximum(chosen - 1, 0))]
            shared = {"place": place(slot), "alive": (NSLOT * index + k < chosen).astype(jnp.float32)}
            for p in range(pairs):
                streams.append([OFF_SLOT * k + OFF_PAIR * p, stream(slot, shared, p)])
        tick = 0
        while streams:
            for entry in list(streams):
                if tick >= entry[0]:
                    try:
                        next(entry[1])
                    except StopIteration:
                        streams.remove(entry)
            tick += 1
        return carry

    lax.fori_loop(0, (chosen + NSLOT - 1) // NSLOT, step, 0)
    if stage == "first":
        return
    half = terms_ref.shape[0] // 2
    rows, step = (strip, strip) if stage == "second" else (quarter, 3 * quarter)
    moves = [(grad.at[:, :, pl.ds(pl.multiple_of(k * step, 8), rows)], out) for k, out in zip((core, 1 - core), outs)]
    if stage == "both":
        moves.append((grad.at[:, :, pl.ds(quarter, strip)], outs[2]))
    copies = [pltpu.make_async_copy(src, dst, out_sems.at[k]) for k, (src, dst) in enumerate(moves)]
    copies.append(pltpu.make_async_copy(terms_ref.at[pl.ds(pl.multiple_of((1 - core) * half, 8), half)], outs[-1], out_sems.at[5]))
    start_all(copies)
    outs[len(moves)][...] = terms_ref[pl.ds(pl.multiple_of(core * half, 8), half), :]
    wait_all(copies)


def half_product(w_ref, which, x):
    n = x.shape[0]
    hi, lo = split(x)
    both = dot(w_ref[which], jnp.concatenate([hi, lo], axis=0))
    return both[:n] + both[n:]


def half_blocks(length):
    n = np.arange(length // 2)
    forward, backward = [], []
    for parity in range(2):
        angle = 2.0 * np.pi * (((2 * n[:, None] + parity) * n[None, :]) % length) / length
        c, s = np.cos(angle) / np.sqrt(length), np.sin(angle) / np.sqrt(length)
        forward.append(np.block([[c, s], [-s, c]]))
        backward.append(np.block([[c.T, -s.T], [s.T, c.T]]))
    out = []
    for mats in (forward, backward):
        both = []
        for w in mats:
            hi, lo = split_np(w)
            both.append(np.block([[hi, hi], [lo, lo]]))
        out.append(np.stack(both))
    return out


def vmem():
    return pl.BlockSpec(memory_space=pltpu.VMEM)


def smem():
    return pl.BlockSpec(memory_space=pltpu.SMEM)


def hbm():
    return pl.BlockSpec(memory_space=pltpu.HBM)


def anywhere():
    return pl.BlockSpec(memory_space=pl.ANY)


def f32(*shape):
    return jax.ShapeDtypeStruct(shape, jnp.float32)


def patterns(stage, scalars, objects, before, amps, probe, tiles, flops):
    length, nmodes = probe.shape[-1], probe.shape[1]
    slots = amps[0].shape[0]
    strip = length
    minus, plus = dft_blocks(length)
    mh, ml = split_np(minus)
    ph, plo = split_np(plus)
    mats = np.concatenate([mh, mh, ml, ph, ph, plo] + [m.reshape(-1, 2 * length) for m in half_blocks(length)], axis=0)
    rows = (2 * nmodes + 1) * length
    half = f32(rows // 2, length)
    frame = (2, tiles, 2 * strip, 128)
    grads = [f32(2, tiles, n, 128) for n in (strip // 2, strip, 3 * strip // 2)]
    out_shape = {
        "first": (f32(*frame), f32(rows, length)),
        "second": (grads[1], grads[1], half, half),
        "both": (grads[0], grads[0], grads[1], half, half),
    }[stage]
    arrays = list(objects) + list(before or ()) + list(amps) + [probe]
    out_specs = tuple(vmem() if shape is half or stage == "first" else anywhere() for shape in out_shape)
    if stage != "first":
        out_specs = out_specs[:-1] + (hbm(),)
    kinds = [hbm() if stage == "both" else anywhere()] * len(objects)
    kinds += [anywhere() if stage == "first" else vmem()] * (len(arrays) - len(objects)) + [hbm()]
    small = [pltpu.VMEM((8, 128), jnp.float32)] * 2
    return pl.pallas_call(
        functools.partial(pattern_kernel, stage),
        out_shape=out_shape,
        in_specs=[smem()] * len(scalars) + kinds,
        out_specs=out_specs,
        scratch_shapes=[pltpu.VMEM(frame, jnp.float32)]
        + (small if stage == "first" else [pltpu.VMEM(frame, jnp.float32), pltpu.VMEM((rows, length), jnp.float32)])
        + [
            pltpu.SMEM((2 * slots + 1,), jnp.int32),
            pltpu.SemaphoreType.DMA((2, tiles)),
            pltpu.SemaphoreType.DMA((6,)),
        ]
        + [pltpu.VMEM(a.shape, a.dtype) for a in [mats] + ([probe, amps[0]] if stage == "first" else [])],
        compiler_params=pltpu.CompilerParams(vmem_limit_bytes=PATTERN_LIMITS[stage]),
        cost_estimate=pl.CostEstimate(flops=flops, bytes_accessed=1024, transcendentals=0),
        name="patterns_" + stage,
    )(*scalars, *arrays, jnp.asarray(mats))


def light_kernel(nsets, strip, first, natural, *refs):
    scals, probe_hbm, refs = refs[:nsets], refs[nsets], refs[nsets + 1 :]
    objects, grads = refs[: 3 if natural else 1], refs[3 if natural else 1 : 5 if natural else 2]
    pre_ref, share_ref, acc, frame, grad, probe_ref, tile_sems, sems = refs[len(objects) + len(grads) :]
    tiles = acc.shape[0]
    rows = frame.shape[2]
    length, nmodes = probe_ref.shape[2], probe_ref.shape[1]
    if natural:
        half = strip // 2
        core = scals[2][PLACE - 1]
        firsts = [pl.multiple_of(k * 3 * half, 8) for k in (core, 1 - core)]
        copies = [c for k in range(2) for c in load_columns(objects[k], frame, firsts[k], half, tile_sems.at[k])]
        copies += load_columns(objects[2], frame, half, strip, tile_sems.at[2])
        moves = [(ref, grad.at[:, :, pl.ds(pl.multiple_of(k * strip, 8), strip)]) for k, ref in zip((core, 1 - core), grads)]
    else:
        copies = []
        moves = [(objects[0].at[:, :, pl.ds(strip // 2, rows)], frame), (grads[0], grad)]
    load = pltpu.make_async_copy(probe_hbm, probe_ref, sems.at[0])
    copies += [pltpu.make_async_copy(src, dst, sems.at[1 + k]) for k, (src, dst) in enumerate(moves)]
    start_all([load] + copies)
    acc[...] = jnp.zeros_like(acc)
    load.wait()
    power = None
    for m in range(nmodes):
        term = probe_ref[0, m] * probe_ref[0, m] + probe_ref[1, m] * probe_ref[1, m]
        power = term if power is None else power + term
    wide0 = jnp.concatenate([power, jnp.zeros_like(power)], axis=1)
    for s in range(nsets):

        def step(slot, carry, s=s):
            row = scals[s][slot] + s * strip
            col = scals[s][16 + slot]
            tile = jnp.minimum(col // 128, tiles - 2)
            wide = pltpu.roll(wide0, col - tile * 128, 1)
            for k in range(2):
                acc[tile + k, pl.ds(row, length), :] += wide[:, k * 128 : (k + 1) * 128]
            return carry

        lax.fori_loop(0, scals[s][32], step, 0)
    wait_all(copies)

    def combine(t, carry):
        share = 1.0 / (acc[t, first : first + rows] + 1.0)
        acc[t, first : first + rows] = share
        for part in range(2):
            frame[part, t] -= grad[part, t] * share
        return carry

    lax.fori_loop(0, tiles, combine, 0)
    stores = [
        pltpu.make_async_copy(frame, pre_ref, sems.at[3]),
        pltpu.make_async_copy(acc.at[:, pl.ds(first, rows)], share_ref, sems.at[4]),
    ]
    start_all(stores)
    wait_all(stores)


def light(scalars, probe, objects, grads, strip, tiles, first, rows):
    natural = len(objects) == 3
    nsets = len(scalars)
    return pl.pallas_call(
        functools.partial(light_kernel, nsets, strip, first, natural),
        out_shape=(f32(2, tiles, rows, 128), f32(tiles, rows, 128)),
        in_specs=[smem()] * nsets + [anywhere()] * (1 + len(objects) + len(grads)),
        out_specs=(anywhere(), anywhere()),
        scratch_shapes=[
            pltpu.VMEM((tiles, (nsets + 1) * strip, 128), jnp.float32),
            pltpu.VMEM((2, tiles, rows, 128), jnp.float32),
            pltpu.VMEM((2, tiles, rows, 128), jnp.float32),
            pltpu.VMEM(probe.shape, jnp.float32),
            pltpu.SemaphoreType.DMA((3, tiles)),
            pltpu.SemaphoreType.DMA((5,)),
        ],
        compiler_params=pltpu.CompilerParams(vmem_limit_bytes=VMEM_LIMIT),
        cost_estimate=pl.CostEstimate(flops=1000, bytes_accessed=1000, transcendentals=0),
        name="light",
    )(*scalars, probe, *objects, *grads)


def meet_kernel(scal_ref, pre, share, cross, chip, out, frame, sems):
    strip = cross.shape[2]
    core = scal_ref[PLACE - 1]

    def tile(t, carry):
        for part in range(2):
            for k, got in ((core, cross), (1 - core, chip)):
                r = pl.ds(pl.multiple_of(k * strip, 8), strip)
                frame[part, t, r, :] = pre[part, t, r, :] - got[part, t] * share[t, r, :]
        pltpu.make_async_copy(frame.at[:, t], out.at[:, t], sems.at[t]).start()
        return carry

    lax.fori_loop(0, frame.shape[1], tile, 0)
    wait_all([pltpu.make_async_copy(frame.at[:, t], out.at[:, t], sems.at[t]) for t in range(frame.shape[1])])


def meet(scalars, pre, share, cross, chip):
    return pl.pallas_call(
        meet_kernel,
        out_shape=f32(*pre.shape),
        in_specs=[smem()] + [vmem()] * 4,
        out_specs=hbm(),
        scratch_shapes=[pltpu.VMEM(pre.shape, jnp.float32), pltpu.SemaphoreType.DMA((pre.shape[1],))],
        compiler_params=pltpu.CompilerParams(vmem_limit_bytes=VMEM_LIMIT),
        cost_estimate=pl.CostEstimate(flops=1000, bytes_accessed=1000, transcendentals=0),
        name="meet",
    )(scalars, pre, share, cross, chip)


def last_kernel(scal_ref, pre, share, cross, chip, out):
    half = cross.shape[2]
    core = scal_ref[PLACE - 1]
    for t in range(pre.shape[1]):
        c = slice(t * 128, (t + 1) * 128)
        for part in range(2):
            for k, got in ((core, cross), (1 - core, chip)):
                r = pl.ds(pl.multiple_of(k * half, 8), half)
                out[part, r, c] = pre[part, t, r, :] - got[part, t] * share[t, r, :]


def last(scalars, pre, share, cross, chip):
    tiles, strip = pre.shape[1:3]

    def block(rows):
        return pl.BlockSpec((2, STEP_TILES, rows, 128), lambda j: (0, j, 0, 0))

    return pl.pallas_call(
        last_kernel,
        out_shape=f32(2, strip, tiles * 128),
        grid=(tiles // STEP_TILES,),
        in_specs=[smem(), block(strip), pl.BlockSpec((STEP_TILES, strip, 128), lambda j: (j, 0, 0)), block(strip // 2), block(strip // 2)],
        out_specs=pl.BlockSpec((2, strip, STEP_TILES * 128), lambda j: (0, 0, j)),
        compiler_params=pltpu.CompilerParams(vmem_limit_bytes=VMEM_LIMIT),
        cost_estimate=pl.CostEstimate(flops=1000, bytes_accessed=1000, transcendentals=0),
        name="last",
    )(scalars, pre, share, cross, chip)


def shift_by(value, steps):
    count = lax.axis_size("dev")
    return lax.ppermute(
        value, "dev", [(i, i + steps) for i in range(count) if 0 <= i + steps < count]
    )


def rotate(value, stride, extent, steps):
    count = lax.axis_size("dev")

    def target(i):
        z = (i // stride) % extent
        return i + ((z + steps) % extent - z) * stride

    return lax.ppermute(value, "dev", [(i, target(i)) for i in range(count)])


def small_call(kernel, out_shape, operands, scratch=()):
    several = isinstance(out_shape, tuple)
    return pl.pallas_call(
        kernel,
        out_shape=out_shape,
        in_specs=[smem()] + [vmem()] * (len(operands) - 1),
        out_specs=(vmem(),) * len(out_shape) if several else vmem(),
        scratch_shapes=list(scratch),
        compiler_params=pltpu.CompilerParams(vmem_limit_bytes=8 * MIB),
        cost_estimate=pl.CostEstimate(flops=1000, bytes_accessed=1000, transcendentals=0),
        name=kernel.__name__,
    )(*operands)


def deal_kernel(scal_ref, keep, got, *outs):
    rows = outs[0].shape[0]
    for k, out in enumerate(outs):
        r = pl.ds(pl.multiple_of(lax.rem(scal_ref[PLACE] + k, len(outs)) * rows, 8), rows)
        out[...] = keep[r, :] + got[r, :]


def gather_kernel(scal_ref, *refs):
    pieces, out = refs[:-1], refs[-1]
    rows, count = pieces[0].shape[0], len(pieces)
    for k, piece in enumerate(pieces):
        r = pl.ds(pl.multiple_of(lax.rem(scal_ref[PLACE] + count - k, count) * rows, 8), rows)
        out[r, :] = piece[...]


def probe_kernel(scal_ref, mine, other, probe, out, summed):
    half = mine.shape[0]
    core = scal_ref[PLACE - 1]
    summed[pl.ds(pl.multiple_of(core * half, 8), half), :] = mine[...]
    summed[pl.ds(pl.multiple_of((1 - core) * half, 8), half), :] = other[...]
    parts, nmodes, length = probe.shape[:3]
    share = 1.0 / (summed[parts * nmodes * length :, :] + 1.0)
    for part in range(parts):
        for m in range(nmodes):
            first = (part * nmodes + m) * length
            out[part, m] = probe[part, m] - summed[first : first + length, :] * share


def ring_sum(own, pieces, stride):
    total = own
    for k, piece in enumerate(pieces):
        total = total + rotate(piece, stride, 4, k + 1)
    return total


def shards(object_field, probe, amplitudes, positions, counts):
    strip, columns = object_field.shape[1:]
    nmodes, length = probe.shape[1], probe.shape[-1]
    half, tiles = strip // 2, columns // 128
    barrier = lax.optimization_barrier
    device = lax.axis_index("dev")
    mine = jnp.concatenate([positions[:, 0] - device * strip, positions[:, 1], counts, (device % 2)[None], (device // 32 % 4)[None]])

    def scattered(keep, send):
        pieces = small_call(deal_kernel, (f32(keep.shape[0] // 4, length),) * 4, (mine, keep, rotate(send, 1, 2, 1)))
        return ring_sum(pieces[0], pieces[1:], 32)

    def gathered(part):
        part = ring_sum(part, (part,) * 3, 2)
        pieces = [part] + [rotate(part, 32, 4, k) for k in (1, 2, 3)]
        return small_call(gather_kernel, f32(4 * part.shape[0], length), [mine] + pieces)

    def moved(probe, half):
        terms = pltpu.VMEM((2 * half.shape[0], length), jnp.float32)
        return small_call(probe_kernel, f32(*probe.shape), (mine, half, rotate(half, 1, 2, 1), probe), (terms,))

    core = device % 2
    count = lax.axis_size("dev")
    chip_down = [(i, i + 1) for i in range(0, count, 2)]
    cross_down = [(i, i + 1) for i in range(1, count - 1, 2)]

    def swap(value, pairs):
        return lax.ppermute(value, "dev", pairs + [(j, i) for i, j in pairs])

    def exchange(cross, chip):
        return swap(cross, cross_down), swap(chip, chip_down)

    extra = jnp.pad(mine.astype(jnp.float32)[None, None], ((0, 1), (0, 7), (0, columns - mine.shape[0])))

    def edge(which):
        return jnp.concatenate([lax.dynamic_slice_in_dim(object_field, which * half, half, 1), extra], axis=1)

    def info(halo):
        return halo[0, half, : mine.shape[0]].astype(jnp.int32)

    cross, chip = exchange(edge(core), edge(1 - core))
    amps_cross = lax.ppermute(amplitudes, "dev", cross_down)
    amps_chip = swap(amplitudes, chip_down)
    second = shift_by(mine, 2)
    from_chip = info(chip)
    amps = (amplitudes, amps_chip)
    before = patterns("first", (mine, jnp.where(core == 0, mine, from_chip)), (chip, object_field), None, amps, probe, tiles, 1000)
    second, cross, amps_cross, before = barrier((second, cross, amps_cross, before))
    from_cross = info(cross)
    chosen = jnp.where(core == 0, from_cross, mine)
    amps = (amplitudes, amps_cross)
    out, inner, keep, send = patterns("second", (mine, chosen), (cross, object_field), before, amps, probe, tiles, 10**9)
    got, got_inner = exchange(out, inner)
    prev = jnp.where(core == 0, from_cross, from_chip)
    following = jnp.where(core == 0, from_chip, from_cross)
    near = (second, prev, mine, following)
    pre, share = light(near, probe, (cross, chip, object_field), (out, inner), strip, tiles, strip + half, 2 * strip)
    got, got_inner, pre, share, part = barrier((got, got_inner, pre, share, scattered(keep, send)))
    frame, part = barrier((meet(mine, pre, share, got, got_inner), ring_sum(part, (part,) * 3, 8)))
    probe = moved(probe, gathered(part))

    amps = (amplitudes, amps_chip, amps_cross)
    out, inner, gmid, keep, send = patterns("both", (mine, prev), (frame,), None, amps, probe, tiles, 10**9)
    got, got_inner = exchange(out, inner)
    pre, share = light((prev, mine), probe, (frame,), (gmid,), strip, tiles, strip, strip)
    got, got_inner, pre, share, part = barrier((got, got_inner, pre, share, scattered(keep, send)))
    current, part = barrier((last(mine, pre, share, got, got_inner), ring_sum(part, (part,) * 3, 8)))
    return (current, moved(probe, gathered(part)))


def solution(mesh):
    placed = (P(None, "dev", None), P(), P("dev", None, None), P("dev", None), P("dev"))
    return jax.shard_map(
        shards, mesh=mesh, in_specs=placed, out_specs=(P(None, "dev", None), P()), check_vma=False
    )
```

```python
import functools

import jax
import jax.numpy as jnp
import ml_dtypes
import numpy as np
from jax import lax
from jax.experimental import pallas as pl
from jax.experimental.pallas import tpu as pltpu
from jax.sharding import PartitionSpec as P

SIGMA = 0.5
NSLOT, OFF_SLOT, OFF_PAIR = 2, 1, 0
STEP_TILES = 4
MIB = 1024 * 1024
PATTERN_LIMITS = {"first": 20 * MIB, "second": 24 * MIB, "both": 30 * MIB}
PLACE = 34
TURNS = (2, 1, 3)
VMEM_LIMIT = 24 * MIB


def split_np(w):
    hi = w.astype(ml_dtypes.bfloat16)
    lo = (w - hi.astype(np.float64)).astype(ml_dtypes.bfloat16)
    return hi, lo


def dft_blocks(length):
    index = np.arange(length)
    angle = 2.0 * np.pi * ((index[:, None] * index[None, :]) % length) / length
    c = np.cos(angle) / np.sqrt(length)
    s = np.sin(angle) / np.sqrt(length)
    minus = np.block([[c, -s], [s, c]])
    plus = np.block([[c, s], [-s, c]])
    return minus, plus


def split(x):
    hi = x.astype(jnp.bfloat16)
    lo = (x - hi.astype(jnp.float32)).astype(jnp.bfloat16)
    return hi, lo


def dot(a, b):
    return lax.dot_general(a, b, (((1,), (0,)), ((), ())), preferred_element_type=jnp.float32)


def right_product(x, w_ref):
    hi, lo = split(x)
    return dot(jnp.concatenate([hi, lo, hi], axis=1), w_ref[...])


def left_product(w_ref, x):
    n = x.shape[0]
    hi, lo = split(x)
    both = dot(w_ref[...], hi)
    return both[:n] + both[n:] + dot(w_ref[:n], lo)


def load_columns(ref, frame, first, rows, sems):
    return [
        pltpu.make_async_copy(ref.at[:, pl.ds(0, rows), pl.ds(t * 128, 128)], frame.at[:, t, pl.ds(first, rows), :], sems.at[t])
        for t in range(frame.shape[1])
    ]


def start_all(copies):
    for copy in copies:
        copy.start()


def wait_all(copies):
    for copy in copies:
        copy.wait()


def pattern_kernel(stage, *refs):
    refs = list(refs)
    take = lambda n: [refs.pop(0) for _ in range(n)]
    scals = take(2)
    objects = take({"first": 2, "second": 2, "both": 1}[stage])
    before = take(2) if stage == "second" else None
    amps = take(3 if stage == "both" else 2)
    probe_hbm, mats_hbm = take(2)
    outs = take({"first": 2, "second": 4, "both": 5}[stage])
    frame, grad, terms_ref, order, tile_sems, out_sems = take(6)
    if stage == "both":
        frame = objects[0]
    core = scals[0][PLACE - 1]
    slots = amps[0].shape[0]
    moves = []
    mats_ref = mats_hbm
    probe_ref = probe_hbm
    if stage == "first":
        grad, terms_ref = outs
        probe_ref, amp_ref = take(2)
        moves.append((probe_hbm, probe_ref))
    size = mats_ref.shape[1]
    rf_ref, rb_ref = (mats_ref.at[pl.ds(3 * size * k, 3 * size)] for k in range(2))
    lf_ref, lb_ref = ([mats_ref.at[pl.ds(size * (6 + 2 * k + n), size)] for n in range(2)] for k in range(2))
    tiles, strip = frame.shape[1], frame.shape[2] // 2
    quarter = strip // 2
    nmodes, length = probe_ref.shape[1], probe_ref.shape[2]

    if stage == "both":
        copies = []
    else:
        where = ((1 - core) if stage == "first" else core) * (3 * quarter)
        copies = load_columns(objects[0], frame, pl.multiple_of(where, 8), quarter, tile_sems.at[0])
        copies += load_columns(objects[1], frame, quarter, strip, tile_sems.at[1])
    copies += [pltpu.make_async_copy(src, dst, out_sems.at[k]) for k, (src, dst) in enumerate(moves)]
    start_all(copies)
    if stage == "first":
        choice = [pltpu.make_async_copy(amp, amp_ref, out_sems.at[5]) for amp in amps]
        for k in range(2):
            pl.when(core == k)(choice[k].start)
        copies.append(choice[0])
    if stage == "second":

        def take_over(t, carry):
            grad[:, t] = before[0][:, t]
            return carry

        lax.fori_loop(0, tiles, take_over, 0)
        terms_ref[...] = before[1][...]
    else:
        grad[...] = jnp.zeros_like(grad)
        terms_ref[...] = jnp.zeros_like(terms_ref)
    owners = {"first": (core,), "second": (1 - core,), "both": (0, 1)}[stage]
    chosen = jnp.int32(0)
    for k, owner in enumerate(owners):
        scal = scals[k if stage == "both" else 1]
        for local in range(slots):
            order[chosen] = k * slots + local
            inside = (local < scal[2 * slots]) & ((scal[local] >= quarter).astype(jnp.int32) == owner)
            chosen = chosen + inside.astype(jnp.int32)
    wait_all(copies)

    def amplitude(slot, k, h):
        def part(ref, index):
            return ref[index, pl.ds(k, h, stride=2), :]

        if stage == "first":
            return part(amp_ref, slot)
        local = slot % slots
        if stage == "second":
            return jnp.where(core == 0, part(amps[1], local), part(amps[0], local))
        others = jnp.where(core == 0, part(amps[2], local), part(amps[1], local))
        return jnp.where(slot < slots, part(amps[0], local), others)

    h = length // 2
    pairs = nmodes // 2

    def place(slot):
        local = slot % slots
        if stage == "both":
            first = slot < slots
            row, col = (jnp.where(first, scals[0][local + k * slots], scals[1][local + k * slots]) for k in range(2))
            row = jnp.where(first, row, row - strip)
        else:
            row, col = (scals[1][local + k * slots] for k in range(2))
            row = row - owners[0] * strip
        tile = jnp.minimum(col // 128, tiles - 2)
        return row + quarter, tile, col - tile * 128

    def stream(slot, shared, p):
        row, tile, shift = shared["place"]
        if p == 0:
            back = lax.rem(256 - shift, 256)

            def cut(part):
                wide = jnp.concatenate([frame[part, tile + k, pl.ds(row, length), :] for k in range(2)], axis=1)
                return pltpu.roll(wide, back, 1)[:, :length]

            shared["x"] = (cut(0), cut(1))
        xr, xi = shared["x"]
        modes = (2 * p, 2 * p + 1)
        waves = []
        for m in modes:
            pr, pi = probe_ref[0, m], probe_ref[1, m]
            waves.append(split(jnp.concatenate([pr * xr - pi * xi, pr * xi + pi * xr], axis=1)))
        yield
        mids = [dot(jnp.concatenate([hi, lo, hi], axis=1), rf_ref[...]) for hi, lo in waves]
        yield
        top = jnp.concatenate([jnp.concatenate([y[:h, :length] for y in mids], axis=1), jnp.concatenate([y[:h, length:] for y in mids], axis=1)], axis=0)
        low = jnp.concatenate([jnp.concatenate([y[h:, :length] for y in mids], axis=1), jnp.concatenate([y[h:, length:] for y in mids], axis=1)], axis=0)
        sums = [jnp.concatenate(split(v), axis=0) for v in (top + low, top - low)]
        yield
        fars = [dot(lf_ref[k][...], v) for k, v in enumerate(sums)]
        yield
        fars = [f[:length] + f[length:] for f in fars]
        sq = [f * f for f in fars]
        sq = [q[:h] + q[h:] for q in sq]
        shared.setdefault("power", []).extend(q[:, k * length : (k + 1) * length] for k in range(2) for q in [jnp.concatenate(sq, axis=0)])
        yield
        while len(shared["power"]) < nmodes:
            yield
        if "weight" not in shared:
            intensity = functools.reduce(lambda a, b: a + b, shared["power"])
            amp = jnp.concatenate([amplitude(slot, k, h) for k in range(2)], axis=0)
            shared["weight"] = (1.0 - amp * lax.rsqrt(intensity + SIGMA)) * shared["alive"]
        w = jnp.concatenate([shared["weight"]] * 2, axis=1)
        ins = [split(f * jnp.concatenate([wk, wk], axis=0)) for f, wk in zip(fars, (w[:h], w[h:]))]
        yield
        u, v = [dot(lb_ref[k][...], jnp.concatenate(x, axis=0)) for k, x in enumerate(ins)]
        yield
        u, v = u[:length] + u[length:], v[:length] + v[length:]
        a, b = u + v, u - v
        ins = []
        for k in range(2):
            c = slice(k * length, (k + 1) * length)
            re = jnp.concatenate([a[:h, c], b[:h, c]], axis=0)
            im = jnp.concatenate([a[h:, c], b[h:, c]], axis=0)
            ins.append(split(jnp.concatenate([re, im], axis=1)))
        yield
        chis = [dot(jnp.concatenate([hi, lo, hi], axis=1), rb_ref[...]) for hi, lo in ins]
        yield
        for m, chi in zip(modes, chis):
            cr, ci = chi[:, :length], chi[:, length:]
            pr, pi = probe_ref[0, m], probe_ref[1, m]
            a = pr * cr + pi * ci
            b = pr * ci - pi * cr
            g = shared.get("g")
            shared["g"] = (a, b) if g is None else (g[0] + a, g[1] + b)
            terms_ref[m * length : (m + 1) * length] += xr * cr + xi * ci
            terms_ref[(nmodes + m) * length : (nmodes + m + 1) * length] += xr * ci - xi * cr
        shared["done"] = shared.get("done", 0) + 1
        if shared["done"] == pairs:
            terms_ref[2 * nmodes * length :] += (xr * xr + xi * xi) * shared["alive"]
            pad = jnp.zeros((length, 128), jnp.float32)
            for part, g in enumerate(shared["g"]):
                wide = pltpu.roll(jnp.concatenate([g, pad], axis=1), shift, 1)
                for k in range(2):
                    grad[part, tile + k, pl.ds(row, length), :] += wide[:, k * 128 : (k + 1) * 128]
        yield

    def step(index, carry):
        streams = []
        for k in range(NSLOT):
            slot = order[jnp.minimum(NSLOT * index + k, jnp.maximum(chosen - 1, 0))]
            shared = {"place": place(slot), "alive": (NSLOT * index + k < chosen).astype(jnp.float32)}
            for p in range(pairs):
                streams.append([OFF_SLOT * k + OFF_PAIR * p, stream(slot, shared, p)])
        tick = 0
        while streams:
            for entry in list(streams):
                if tick >= entry[0]:
                    try:
                        next(entry[1])
                    except StopIteration:
                        streams.remove(entry)
            tick += 1
        return carry

    lax.fori_loop(0, (chosen + NSLOT - 1) // NSLOT, step, 0)
    if stage == "first":
        return
    half = terms_ref.shape[0] // 2
    rows, step = (strip, strip) if stage == "second" else (quarter, 3 * quarter)
    moves = [(grad.at[:, :, pl.ds(pl.multiple_of(k * step, 8), rows)], out) for k, out in zip((core, 1 - core), outs)]
    if stage == "both":
        moves.append((grad.at[:, :, pl.ds(quarter, strip)], outs[2]))
    copies = [pltpu.make_async_copy(src, dst, out_sems.at[k]) for k, (src, dst) in enumerate(moves)]
    copies.append(pltpu.make_async_copy(terms_ref.at[pl.ds(pl.multiple_of((1 - core) * half, 8), half)], outs[-1], out_sems.at[5]))
    start_all(copies)
    outs[len(moves)][...] = terms_ref[pl.ds(pl.multiple_of(core * half, 8), half), :]
    wait_all(copies)


def half_product(w_ref, which, x):
    n = x.shape[0]
    hi, lo = split(x)
    both = dot(w_ref[which], jnp.concatenate([hi, lo], axis=0))
    return both[:n] + both[n:]


def half_blocks(length):
    n = np.arange(length // 2)
    forward, backward = [], []
    for parity in range(2):
        angle = 2.0 * np.pi * (((2 * n[:, None] + parity) * n[None, :]) % length) / length
        c, s = np.cos(angle) / np.sqrt(length), np.sin(angle) / np.sqrt(length)
        forward.append(np.block([[c, s], [-s, c]]))
        backward.append(np.block([[c.T, -s.T], [s.T, c.T]]))
    out = []
    for mats in (forward, backward):
        both = []
        for w in mats:
            hi, lo = split_np(w)
            both.append(np.block([[hi, hi], [lo, lo]]))
        out.append(np.stack(both))
    return out


def vmem():
    return pl.BlockSpec(memory_space=pltpu.VMEM)


def smem():
    return pl.BlockSpec(memory_space=pltpu.SMEM)


def hbm():
    return pl.BlockSpec(memory_space=pltpu.HBM)


def anywhere():
    return pl.BlockSpec(memory_space=pl.ANY)


def f32(*shape):
    return jax.ShapeDtypeStruct(shape, jnp.float32)


def patterns(stage, scalars, objects, before, amps, probe, tiles, flops):
    length, nmodes = probe.shape[-1], probe.shape[1]
    slots = amps[0].shape[0]
    strip = length
    minus, plus = dft_blocks(length)
    mh, ml = split_np(minus)
    ph, plo = split_np(plus)
    mats = np.concatenate([mh, mh, ml, ph, ph, plo] + [m.reshape(-1, 2 * length) for m in half_blocks(length)], axis=0)
    rows = (2 * nmodes + 1) * length
    half = f32(rows // 2, length)
    frame = (2, tiles, 2 * strip, 128)
    grads = [f32(2, tiles, n, 128) for n in (strip // 2, strip, 3 * strip // 2)]
    out_shape = {
        "first": (f32(*frame), f32(rows, length)),
        "second": (grads[1], grads[1], half, half),
        "both": (grads[0], grads[0], grads[1], half, half),
    }[stage]
    arrays = list(objects) + list(before or ()) + list(amps) + [probe]
    out_specs = tuple(vmem() if shape is half or stage == "first" else anywhere() for shape in out_shape)
    if stage != "first":
        out_specs = out_specs[:-1] + (hbm(),)
    kinds = [vmem() if stage == "both" else anywhere()] * len(objects)
    kinds += [anywhere() if stage == "first" else vmem()] * (len(arrays) - len(objects)) + [vmem()]
    small = [pltpu.VMEM((8, 128), jnp.float32)] * 2
    return pl.pallas_call(
        functools.partial(pattern_kernel, stage),
        out_shape=out_shape,
        in_specs=[smem()] * len(scalars) + kinds,
        out_specs=out_specs,
        scratch_shapes=[pltpu.VMEM((8, 128) if stage == "both" else frame, jnp.float32)]
        + (small if stage == "first" else [pltpu.VMEM(frame, jnp.float32), pltpu.VMEM((rows, length), jnp.float32)])
        + [
            pltpu.SMEM((2 * slots + 1,), jnp.int32),
            pltpu.SemaphoreType.DMA((2, tiles)),
            pltpu.SemaphoreType.DMA((6,)),
        ]
        + ([pltpu.VMEM(a.shape, a.dtype) for a in (probe, amps[0])] if stage == "first" else []),
        compiler_params=pltpu.CompilerParams(vmem_limit_bytes=PATTERN_LIMITS[stage]),
        cost_estimate=pl.CostEstimate(flops=flops, bytes_accessed=1024, transcendentals=0),
        name="patterns_" + stage,
    )(*scalars, *arrays, jnp.asarray(mats))


def light_kernel(nsets, strip, first, natural, *refs):
    scals, probe_hbm, refs = refs[:nsets], refs[nsets], refs[nsets + 1 :]
    objects, grads = refs[: 3 if natural else 1], refs[3 if natural else 1 : 5 if natural else 2]
    pre_ref, share_ref, acc, frame, grad, probe_ref, tile_sems, sems = refs[len(objects) + len(grads) :]
    tiles = acc.shape[0]
    rows = frame.shape[2]
    length, nmodes = probe_ref.shape[2], probe_ref.shape[1]
    if natural:
        half = strip // 2
        core = scals[2][PLACE - 1]
        firsts = [pl.multiple_of(k * 3 * half, 8) for k in (core, 1 - core)]
        copies = [c for k in range(2) for c in load_columns(objects[k], frame, firsts[k], half, tile_sems.at[k])]
        copies += load_columns(objects[2], frame, half, strip, tile_sems.at[2])
        moves = [(ref, grad.at[:, :, pl.ds(pl.multiple_of(k * strip, 8), strip)]) for k, ref in zip((core, 1 - core), grads)]
    else:
        copies = []
        moves = [(objects[0].at[:, :, pl.ds(strip // 2, rows)], frame), (grads[0], grad)]
    load = pltpu.make_async_copy(probe_hbm, probe_ref, sems.at[0])
    copies += [pltpu.make_async_copy(src, dst, sems.at[1 + k]) for k, (src, dst) in enumerate(moves)]
    start_all([load] + copies)
    acc[...] = jnp.zeros_like(acc)
    load.wait()
    power = None
    for m in range(nmodes):
        term = probe_ref[0, m] * probe_ref[0, m] + probe_ref[1, m] * probe_ref[1, m]
        power = term if power is None else power + term
    wide0 = jnp.concatenate([power, jnp.zeros_like(power)], axis=1)
    for s in range(nsets):

        def step(slot, carry, s=s):
            row = scals[s][slot] + s * strip
            col = scals[s][16 + slot]
            tile = jnp.minimum(col // 128, tiles - 2)
            wide = pltpu.roll(wide0, col - tile * 128, 1)
            for k in range(2):
                acc[tile + k, pl.ds(row, length), :] += wide[:, k * 128 : (k + 1) * 128]
            return carry

        lax.fori_loop(0, scals[s][32], step, 0)
    wait_all(copies)

    def combine(t, carry):
        share = 1.0 / (acc[t, first : first + rows] + 1.0)
        share_ref[t] = share
        for part in range(2):
            pre_ref[part, t] = frame[part, t] - grad[part, t] * share
        return carry

    lax.fori_loop(0, tiles, combine, 0)


def light(scalars, probe, objects, grads, strip, tiles, first, rows):
    natural = len(objects) == 3
    nsets = len(scalars)
    return pl.pallas_call(
        functools.partial(light_kernel, nsets, strip, first, natural),
        out_shape=(f32(2, tiles, rows, 128), f32(tiles, rows, 128)),
        in_specs=[smem()] * nsets + [anywhere()] * (1 + len(objects) + len(grads)),
        out_specs=(vmem(), vmem()),
        scratch_shapes=[
            pltpu.VMEM((tiles, (nsets + 1) * strip, 128), jnp.float32),
            pltpu.VMEM((2, tiles, rows, 128), jnp.float32),
            pltpu.VMEM((2, tiles, rows, 128), jnp.float32),
            pltpu.VMEM(probe.shape, jnp.float32),
            pltpu.SemaphoreType.DMA((3, tiles)),
            pltpu.SemaphoreType.DMA((5,)),
        ],
        compiler_params=pltpu.CompilerParams(vmem_limit_bytes=VMEM_LIMIT),
        cost_estimate=pl.CostEstimate(flops=1000, bytes_accessed=1000, transcendentals=0),
        name="light",
    )(*scalars, probe, *objects, *grads)


def meet_kernel(scal_ref, pre, share, cross, chip, out):
    strip = cross.shape[2]
    core = scal_ref[PLACE - 1]

    def tile(t, carry):
        for part in range(2):
            for k, got in ((core, cross), (1 - core, chip)):
                r = pl.ds(pl.multiple_of(k * strip, 8), strip)
                out[part, t, r, :] = pre[part, t, r, :] - got[part, t] * share[t, r, :]
        return carry

    lax.fori_loop(0, out.shape[1], tile, 0)


def meet(scalars, pre, share, cross, chip):
    return pl.pallas_call(
        meet_kernel,
        out_shape=f32(*pre.shape),
        in_specs=[smem()] + [vmem()] * 4,
        out_specs=vmem(),
        compiler_params=pltpu.CompilerParams(vmem_limit_bytes=VMEM_LIMIT),
        cost_estimate=pl.CostEstimate(flops=1000, bytes_accessed=1000, transcendentals=0),
        name="meet",
    )(scalars, pre, share, cross, chip)


def last_kernel(scal_ref, pre, share, cross, chip, out):
    half = cross.shape[2]
    core = scal_ref[PLACE - 1]
    for t in range(pre.shape[1]):
        c = slice(t * 128, (t + 1) * 128)
        for part in range(2):
            for k, got in ((core, cross), (1 - core, chip)):
                r = pl.ds(pl.multiple_of(k * half, 8), half)
                out[part, r, c] = pre[part, t, r, :] - got[part, t] * share[t, r, :]


def last(scalars, pre, share, cross, chip):
    tiles, strip = pre.shape[1:3]

    def block(rows):
        return pl.BlockSpec((2, STEP_TILES, rows, 128), lambda j: (0, j, 0, 0))

    return pl.pallas_call(
        last_kernel,
        out_shape=f32(2, strip, tiles * 128),
        grid=(tiles // STEP_TILES,),
        in_specs=[smem(), block(strip), pl.BlockSpec((STEP_TILES, strip, 128), lambda j: (j, 0, 0)), block(strip // 2), block(strip // 2)],
        out_specs=pl.BlockSpec((2, strip, STEP_TILES * 128), lambda j: (0, 0, j)),
        compiler_params=pltpu.CompilerParams(vmem_limit_bytes=VMEM_LIMIT),
        cost_estimate=pl.CostEstimate(flops=1000, bytes_accessed=1000, transcendentals=0),
        name="last",
    )(scalars, pre, share, cross, chip)


def shift_by(value, steps):
    count = lax.axis_size("dev")
    return lax.ppermute(
        value, "dev", [(i, i + steps) for i in range(count) if 0 <= i + steps < count]
    )


def rotate(value, stride, extent, steps):
    count = lax.axis_size("dev")

    def target(i):
        z = (i // stride) % extent
        return i + ((z + steps) % extent - z) * stride

    return lax.ppermute(value, "dev", [(i, target(i)) for i in range(count)])


def small_call(kernel, out_shape, operands, scratch=()):
    several = isinstance(out_shape, tuple)
    return pl.pallas_call(
        kernel,
        out_shape=out_shape,
        in_specs=[smem()] + [vmem()] * (len(operands) - 1),
        out_specs=(vmem(),) * len(out_shape) if several else vmem(),
        scratch_shapes=list(scratch),
        compiler_params=pltpu.CompilerParams(vmem_limit_bytes=8 * MIB),
        cost_estimate=pl.CostEstimate(flops=1000, bytes_accessed=1000, transcendentals=0),
        name=kernel.__name__,
    )(*operands)


def deal_kernel(scal_ref, keep, got, *outs):
    rows = outs[0].shape[0]
    for k, out in enumerate(outs):
        r = pl.ds(pl.multiple_of(lax.rem(scal_ref[PLACE] + k, len(outs)) * rows, 8), rows)
        out[...] = keep[r, :] + got[r, :]


def gather_kernel(scal_ref, *refs):
    pieces, out = refs[:-1], refs[-1]
    rows, count = pieces[0].shape[0], len(pieces)
    for k, piece in zip((0,) + TURNS, pieces):
        r = pl.ds(pl.multiple_of(lax.rem(scal_ref[PLACE] + count - k, count) * rows, 8), rows)
        out[r, :] = piece[...]


def probe_kernel(scal_ref, mine, other, probe, out, summed):
    half = mine.shape[0]
    core = scal_ref[PLACE - 1]
    summed[pl.ds(pl.multiple_of(core * half, 8), half), :] = mine[...]
    summed[pl.ds(pl.multiple_of((1 - core) * half, 8), half), :] = other[...]
    parts, nmodes, length = probe.shape[:3]
    share = 1.0 / (summed[parts * nmodes * length :, :] + 1.0)
    for part in range(parts):
        for m in range(nmodes):
            first = (part * nmodes + m) * length
            out[part, m] = probe[part, m] - summed[first : first + length, :] * share


def ring_sum(own, pieces, stride):
    total = own
    for k in TURNS:
        total = total + rotate(pieces[k - 1], stride, 4, k)
    return total


def shards(object_field, probe, amplitudes, positions, counts):
    strip, columns = object_field.shape[1:]
    nmodes, length = probe.shape[1], probe.shape[-1]
    half, tiles = strip // 2, columns // 128
    barrier = lax.optimization_barrier
    device = lax.axis_index("dev")
    mine = jnp.concatenate([positions[:, 0] - device * strip, positions[:, 1], counts, (device % 2)[None], (device // 32 % 4)[None]])

    def scattered(keep, send):
        pieces = small_call(deal_kernel, (f32(keep.shape[0] // 4, length),) * 4, (mine, keep, rotate(send, 1, 2, 1)))
        return ring_sum(pieces[0], pieces[1:], 32)

    def gathered(part):
        part = ring_sum(part, (part,) * 3, 2)
        pieces = [part] + [rotate(part, 32, 4, k) for k in TURNS]
        return small_call(gather_kernel, f32(4 * part.shape[0], length), [mine] + pieces)

    def moved(probe, half):
        terms = pltpu.VMEM((2 * half.shape[0], length), jnp.float32)
        return small_call(probe_kernel, f32(*probe.shape), (mine, half, rotate(half, 1, 2, 1), probe), (terms,))

    core = device % 2
    count = lax.axis_size("dev")
    chip_down = [(i, i + 1) for i in range(0, count, 2)]
    cross_down = [(i, i + 1) for i in range(1, count - 1, 2)]

    def swap(value, pairs):
        return lax.ppermute(value, "dev", pairs + [(j, i) for i, j in pairs])

    def exchange(cross, chip):
        return swap(cross, cross_down), swap(chip, chip_down)

    extra = jnp.pad(mine.astype(jnp.float32)[None, None], ((0, 1), (0, 7), (0, columns - mine.shape[0])))

    def edge(which):
        return jnp.concatenate([lax.dynamic_slice_in_dim(object_field, which * half, half, 1), extra], axis=1)

    def info(halo):
        return halo[0, half, : mine.shape[0]].astype(jnp.int32)

    cross, chip = exchange(edge(core), edge(1 - core))
    amps_cross = lax.ppermute(amplitudes, "dev", cross_down)
    amps_chip = swap(amplitudes, chip_down)
    second = shift_by(mine, 2)
    from_chip = info(chip)
    amps = (amplitudes, amps_chip)
    before = patterns("first", (mine, jnp.where(core == 0, mine, from_chip)), (chip, object_field), None, amps, probe, tiles, 1000)
    second, cross, amps_cross, before = barrier((second, cross, amps_cross, before))
    from_cross = info(cross)
    chosen = jnp.where(core == 0, from_cross, mine)
    amps = (amplitudes, amps_cross)
    out, inner, keep, send = patterns("second", (mine, chosen), (cross, object_field), before, amps, probe, tiles, 10**9)
    got, got_inner = exchange(out, inner)
    prev = jnp.where(core == 0, from_cross, from_chip)
    following = jnp.where(core == 0, from_chip, from_cross)
    near = (second, prev, mine, following)
    pre, share = light(near, probe, (cross, chip, object_field), (out, inner), strip, tiles, strip + half, 2 * strip)
    got, got_inner, pre, share, part = barrier((got, got_inner, pre, share, scattered(keep, send)))
    frame, part = barrier((meet(mine, pre, share, got, got_inner), ring_sum(part, (part,) * 3, 8)))
    probe = moved(probe, gathered(part))

    amps = (amplitudes, amps_chip, amps_cross)
    out, inner, gmid, keep, send = patterns("both", (mine, prev), (frame,), None, amps, probe, tiles, 10**9)
    got, got_inner = exchange(out, inner)
    pre, share = light((prev, mine), probe, (frame,), (gmid,), strip, tiles, strip, strip)
    got, got_inner, pre, share, part = barrier((got, got_inner, pre, share, scattered(keep, send)))
    current, part = barrier((last(mine, pre, share, got, got_inner), ring_sum(part, (part,) * 3, 8)))
    return (current, moved(probe, gathered(part)))


def solution(mesh):
    placed = (P(None, "dev", None), P(), P("dev", None, None), P("dev", None), P("dev"))
    return jax.shard_map(
        shards, mesh=mesh, in_specs=placed, out_specs=(P(None, "dev", None), P()), check_vma=False
    )
```

```python
import functools

import jax
import jax.numpy as jnp
import ml_dtypes
import numpy as np
from jax import lax
from jax.experimental import pallas as pl
from jax.experimental.pallas import tpu as pltpu
from jax.sharding import PartitionSpec as P

SIGMA = 0.5
NSLOT, OFF_SLOT, OFF_PAIR = 2, 1, 0
STEP_TILES = 4
MIB = 1024 * 1024
PATTERN_LIMITS = {"first": 20 * MIB, "second": 24 * MIB, "both": 30 * MIB}
PLACE = 34
TURNS = (2, 1, 3)
VMEM_LIMIT = 24 * MIB


def split_np(w):
    hi = w.astype(ml_dtypes.bfloat16)
    lo = (w - hi.astype(np.float64)).astype(ml_dtypes.bfloat16)
    return hi, lo


def dft_blocks(length):
    index = np.arange(length)
    angle = 2.0 * np.pi * ((index[:, None] * index[None, :]) % length) / length
    c = np.cos(angle) / np.sqrt(length)
    s = np.sin(angle) / np.sqrt(length)
    minus = np.block([[c, -s], [s, c]])
    plus = np.block([[c, s], [-s, c]])
    return minus, plus


def split(x):
    hi = x.astype(jnp.bfloat16)
    lo = (x - hi.astype(jnp.float32)).astype(jnp.bfloat16)
    return hi, lo


def dot(a, b):
    return lax.dot_general(a, b, (((1,), (0,)), ((), ())), preferred_element_type=jnp.float32)


def right_product(x, w_ref):
    hi, lo = split(x)
    return dot(jnp.concatenate([hi, lo, hi], axis=1), w_ref[...])


def left_product(w_ref, x):
    n = x.shape[0]
    hi, lo = split(x)
    both = dot(w_ref[...], hi)
    return both[:n] + both[n:] + dot(w_ref[:n], lo)


def load_columns(ref, frame, first, rows, sems):
    return [
        pltpu.make_async_copy(ref.at[:, pl.ds(0, rows), pl.ds(t * 128, 128)], frame.at[:, t, pl.ds(first, rows), :], sems.at[t])
        for t in range(frame.shape[1])
    ]


def start_all(copies):
    for copy in copies:
        copy.start()


def wait_all(copies):
    for copy in copies:
        copy.wait()


def pattern_kernel(stage, *refs):
    refs = list(refs)
    take = lambda n: [refs.pop(0) for _ in range(n)]
    scals = take(2)
    objects = take({"first": 2, "second": 2, "both": 1}[stage])
    before = take(2) if stage == "second" else None
    amps = take(3 if stage == "both" else 2)
    probe_hbm, mats_hbm = take(2)
    outs = take({"first": 2, "second": 4, "both": 5}[stage])
    frame, grad, terms_ref, order, tile_sems, out_sems = take(6)
    if stage == "both":
        frame = objects[0]
    core = scals[0][PLACE - 1]
    slots = amps[0].shape[0]
    moves = []
    mats_ref = mats_hbm
    probe_ref = probe_hbm
    if stage == "first":
        grad, terms_ref = outs
        probe_ref, amp_ref = take(2)
        moves.append((probe_hbm, probe_ref))
    size = mats_ref.shape[1]
    rf_ref, rb_ref = (mats_ref.at[pl.ds(3 * size * k, 3 * size)] for k in range(2))
    lf_ref, lb_ref = ([mats_ref.at[pl.ds(size * (6 + 2 * k + n), size)] for n in range(2)] for k in range(2))
    tiles, strip = frame.shape[1], frame.shape[2] // 2
    quarter = strip // 2
    nmodes, length = probe_ref.shape[1], probe_ref.shape[2]

    if stage == "both":
        copies = []
    else:
        where = ((1 - core) if stage == "first" else core) * (3 * quarter)
        copies = load_columns(objects[0], frame, pl.multiple_of(where, 8), quarter, tile_sems.at[0])
        copies += load_columns(objects[1], frame, quarter, strip, tile_sems.at[1])
    copies += [pltpu.make_async_copy(src, dst, out_sems.at[k]) for k, (src, dst) in enumerate(moves)]
    start_all(copies)
    if stage == "first":
        choice = [pltpu.make_async_copy(amp, amp_ref, out_sems.at[5]) for amp in amps]
        for k in range(2):
            pl.when(core == k)(choice[k].start)
        copies.append(choice[0])
    if stage == "second":

        def take_over(t, carry):
            grad[:, t] = before[0][:, t]
            return carry

        lax.fori_loop(0, tiles, take_over, 0)
        terms_ref[...] = before[1][...]
    else:
        grad[...] = jnp.zeros_like(grad)
        terms_ref[...] = jnp.zeros_like(terms_ref)
    owners = {"first": (core,), "second": (1 - core,), "both": (0, 1)}[stage]
    chosen = jnp.int32(0)
    for k, owner in enumerate(owners):
        scal = scals[k if stage == "both" else 1]
        for local in range(slots):
            order[chosen] = k * slots + local
            inside = (local < scal[2 * slots]) & ((scal[local] >= quarter).astype(jnp.int32) == owner)
            chosen = chosen + inside.astype(jnp.int32)
    wait_all(copies)

    def amplitude(slot, k, h):
        def part(ref, index):
            return ref[index, pl.ds(k, h, stride=2), :]

        if stage == "first":
            return part(amp_ref, slot)
        local = slot % slots
        if stage == "second":
            return jnp.where(core == 0, part(amps[1], local), part(amps[0], local))
        others = jnp.where(core == 0, part(amps[2], local), part(amps[1], local))
        return jnp.where(slot < slots, part(amps[0], local), others)

    h = length // 2
    pairs = nmodes // 2

    def place(slot):
        local = slot % slots
        if stage == "both":
            first = slot < slots
            row, col = (jnp.where(first, scals[0][local + k * slots], scals[1][local + k * slots]) for k in range(2))
            row = jnp.where(first, row, row - strip)
        else:
            row, col = (scals[1][local + k * slots] for k in range(2))
            row = row - owners[0] * strip
        tile = jnp.minimum(col // 128, tiles - 2)
        return row + quarter, tile, col - tile * 128

    def stream(slot, shared, p):
        row, tile, shift = shared["place"]
        if p == 0:
            back = lax.rem(256 - shift, 256)

            def cut(part):
                wide = jnp.concatenate([frame[part, tile + k, pl.ds(row, length), :] for k in range(2)], axis=1)
                return pltpu.roll(wide, back, 1)[:, :length]

            shared["x"] = (cut(0), cut(1))
        xr, xi = shared["x"]
        modes = (2 * p, 2 * p + 1)
        waves = []
        for m in modes:
            pr, pi = probe_ref[0, m], probe_ref[1, m]
            waves.append(split(jnp.concatenate([pr * xr - pi * xi, pr * xi + pi * xr], axis=1)))
        yield
        mids = [dot(jnp.concatenate([hi, lo, hi], axis=1), rf_ref[...]) for hi, lo in waves]
        yield
        top = jnp.concatenate([jnp.concatenate([y[:h, :length] for y in mids], axis=1), jnp.concatenate([y[:h, length:] for y in mids], axis=1)], axis=0)
        low = jnp.concatenate([jnp.concatenate([y[h:, :length] for y in mids], axis=1), jnp.concatenate([y[h:, length:] for y in mids], axis=1)], axis=0)
        sums = [jnp.concatenate(split(v), axis=0) for v in (top + low, top - low)]
        yield
        fars = [dot(lf_ref[k][...], v) for k, v in enumerate(sums)]
        yield
        fars = [f[:length] + f[length:] for f in fars]
        sq = [f * f for f in fars]
        sq = [q[:h] + q[h:] for q in sq]
        shared.setdefault("power", []).extend(q[:, k * length : (k + 1) * length] for k in range(2) for q in [jnp.concatenate(sq, axis=0)])
        yield
        while len(shared["power"]) < nmodes:
            yield
        if "weight" not in shared:
            intensity = functools.reduce(lambda a, b: a + b, shared["power"])
            amp = jnp.concatenate([amplitude(slot, k, h) for k in range(2)], axis=0)
            shared["weight"] = (1.0 - amp * lax.rsqrt(intensity + SIGMA))
        w = jnp.concatenate([shared["weight"]] * 2, axis=1)
        ins = [split(f * jnp.concatenate([wk, wk], axis=0)) for f, wk in zip(fars, (w[:h], w[h:]))]
        yield
        u, v = [dot(lb_ref[k][...], jnp.concatenate(x, axis=0)) for k, x in enumerate(ins)]
        yield
        u, v = u[:length] + u[length:], v[:length] + v[length:]
        a, b = u + v, u - v
        ins = []
        for k in range(2):
            c = slice(k * length, (k + 1) * length)
            re = jnp.concatenate([a[:h, c], b[:h, c]], axis=0)
            im = jnp.concatenate([a[h:, c], b[h:, c]], axis=0)
            ins.append(split(jnp.concatenate([re, im], axis=1)))
        yield
        chis = [dot(jnp.concatenate([hi, lo, hi], axis=1), rb_ref[...]) for hi, lo in ins]
        yield
        for m, chi in zip(modes, chis):
            cr, ci = chi[:, :length], chi[:, length:]
            pr, pi = probe_ref[0, m], probe_ref[1, m]
            a = pr * cr + pi * ci
            b = pr * ci - pi * cr
            g = shared.get("g")
            shared["g"] = (a, b) if g is None else (g[0] + a, g[1] + b)
            terms_ref[m * length : (m + 1) * length] += xr * cr + xi * ci
            terms_ref[(nmodes + m) * length : (nmodes + m + 1) * length] += xr * ci - xi * cr
        shared["done"] = shared.get("done", 0) + 1
        if shared["done"] == pairs:
            terms_ref[2 * nmodes * length :] += (xr * xr + xi * xi)
            pad = jnp.zeros((length, 128), jnp.float32)
            for part, g in enumerate(shared["g"]):
                wide = pltpu.roll(jnp.concatenate([g, pad], axis=1), shift, 1)
                for k in range(2):
                    grad[part, tile + k, pl.ds(row, length), :] += wide[:, k * 128 : (k + 1) * 128]
        yield

    def work(first, number):
        streams = []
        for k in range(number):
            slot = order[first + k]
            shared = {"place": place(slot)}
            for p in range(pairs):
                streams.append([OFF_SLOT * k + OFF_PAIR * p, stream(slot, shared, p)])
        tick = 0
        while streams:
            for entry in list(streams):
                if tick >= entry[0]:
                    try:
                        next(entry[1])
                    except StopIteration:
                        streams.remove(entry)
            tick += 1

    def step(index, carry):
        work(NSLOT * index, NSLOT)
        return carry

    def odd_one(index, carry):
        work(chosen - 1, 1)
        return carry

    lax.fori_loop(0, chosen // NSLOT, step, 0)
    lax.fori_loop(0, lax.rem(chosen, NSLOT), odd_one, 0)
    if stage == "first":
        return
    half = terms_ref.shape[0] // 2
    rows, step = (strip, strip) if stage == "second" else (quarter, 3 * quarter)
    moves = [(grad.at[:, :, pl.ds(pl.multiple_of(k * step, 8), rows)], out) for k, out in zip((core, 1 - core), outs)]
    if stage == "both":
        moves.append((grad.at[:, :, pl.ds(quarter, strip)], outs[2]))
    copies = [pltpu.make_async_copy(src, dst, out_sems.at[k]) for k, (src, dst) in enumerate(moves)]
    copies.append(pltpu.make_async_copy(terms_ref.at[pl.ds(pl.multiple_of((1 - core) * half, 8), half)], outs[-1], out_sems.at[5]))
    start_all(copies)
    outs[len(moves)][...] = terms_ref[pl.ds(pl.multiple_of(core * half, 8), half), :]
    wait_all(copies)


def half_product(w_ref, which, x):
    n = x.shape[0]
    hi, lo = split(x)
    both = dot(w_ref[which], jnp.concatenate([hi, lo], axis=0))
    return both[:n] + both[n:]


def half_blocks(length):
    n = np.arange(length // 2)
    forward, backward = [], []
    for parity in range(2):
        angle = 2.0 * np.pi * (((2 * n[:, None] + parity) * n[None, :]) % length) / length
        c, s = np.cos(angle) / np.sqrt(length), np.sin(angle) / np.sqrt(length)
        forward.append(np.block([[c, s], [-s, c]]))
        backward.append(np.block([[c.T, -s.T], [s.T, c.T]]))
    out = []
    for mats in (forward, backward):
        both = []
        for w in mats:
            hi, lo = split_np(w)
            both.append(np.block([[hi, hi], [lo, lo]]))
        out.append(np.stack(both))
    return out


def vmem():
    return pl.BlockSpec(memory_space=pltpu.VMEM)


def smem():
    return pl.BlockSpec(memory_space=pltpu.SMEM)


def hbm():
    return pl.BlockSpec(memory_space=pltpu.HBM)


def anywhere():
    return pl.BlockSpec(memory_space=pl.ANY)


def f32(*shape):
    return jax.ShapeDtypeStruct(shape, jnp.float32)


def patterns(stage, scalars, objects, before, amps, probe, tiles, flops):
    length, nmodes = probe.shape[-1], probe.shape[1]
    slots = amps[0].shape[0]
    strip = length
    minus, plus = dft_blocks(length)
    mh, ml = split_np(minus)
    ph, plo = split_np(plus)
    mats = np.concatenate([mh, mh, ml, ph, ph, plo] + [m.reshape(-1, 2 * length) for m in half_blocks(length)], axis=0)
    rows = (2 * nmodes + 1) * length
    half = f32(rows // 2, length)
    frame = (2, tiles, 2 * strip, 128)
    grads = [f32(2, tiles, n, 128) for n in (strip // 2, strip, 3 * strip // 2)]
    out_shape = {
        "first": (f32(*frame), f32(rows, length)),
        "second": (grads[1], grads[1], half, half),
        "both": (grads[0], grads[0], grads[1], half, half),
    }[stage]
    arrays = list(objects) + list(before or ()) + list(amps) + [probe]
    out_specs = tuple(vmem() if shape is half or stage == "first" else anywhere() for shape in out_shape)
    if stage != "first":
        out_specs = out_specs[:-1] + (hbm(),)
    kinds = [vmem() if stage == "both" else anywhere()] * len(objects)
    kinds += [anywhere() if stage == "first" else vmem()] * (len(arrays) - len(objects)) + [vmem()]
    small = [pltpu.VMEM((8, 128), jnp.float32)] * 2
    return pl.pallas_call(
        functools.partial(pattern_kernel, stage),
        out_shape=out_shape,
        in_specs=[smem()] * len(scalars) + kinds,
        out_specs=out_specs,
        scratch_shapes=[pltpu.VMEM((8, 128) if stage == "both" else frame, jnp.float32)]
        + (small if stage == "first" else [pltpu.VMEM(frame, jnp.float32), pltpu.VMEM((rows, length), jnp.float32)])
        + [
            pltpu.SMEM((2 * slots + 1,), jnp.int32),
            pltpu.SemaphoreType.DMA((2, tiles)),
            pltpu.SemaphoreType.DMA((6,)),
        ]
        + ([pltpu.VMEM(a.shape, a.dtype) for a in (probe, amps[0])] if stage == "first" else []),
        compiler_params=pltpu.CompilerParams(vmem_limit_bytes=PATTERN_LIMITS[stage]),
        cost_estimate=pl.CostEstimate(flops=flops, bytes_accessed=1024, transcendentals=0),
        name="patterns_" + stage,
    )(*scalars, *arrays, jnp.asarray(mats))


def light_kernel(nsets, strip, first, natural, *refs):
    scals, probe_hbm, refs = refs[:nsets], refs[nsets], refs[nsets + 1 :]
    objects, grads = refs[: 3 if natural else 1], refs[3 if natural else 1 : 5 if natural else 2]
    pre_ref, share_ref, acc, frame, grad, probe_ref, tile_sems, sems = refs[len(objects) + len(grads) :]
    tiles = acc.shape[0]
    rows = frame.shape[2]
    length, nmodes = probe_ref.shape[2], probe_ref.shape[1]
    if natural:
        half = strip // 2
        core = scals[2][PLACE - 1]
        firsts = [pl.multiple_of(k * 3 * half, 8) for k in (core, 1 - core)]
        copies = [c for k in range(2) for c in load_columns(objects[k], frame, firsts[k], half, tile_sems.at[k])]
        copies += load_columns(objects[2], frame, half, strip, tile_sems.at[2])
        moves = [(ref, grad.at[:, :, pl.ds(pl.multiple_of(k * strip, 8), strip)]) for k, ref in zip((core, 1 - core), grads)]
    else:
        copies = []
        moves = [(objects[0].at[:, :, pl.ds(strip // 2, rows)], frame), (grads[0], grad)]
    load = pltpu.make_async_copy(probe_hbm, probe_ref, sems.at[0])
    copies += [pltpu.make_async_copy(src, dst, sems.at[1 + k]) for k, (src, dst) in enumerate(moves)]
    start_all([load] + copies)
    acc[...] = jnp.zeros_like(acc)
    load.wait()
    power = None
    for m in range(nmodes):
        term = probe_ref[0, m] * probe_ref[0, m] + probe_ref[1, m] * probe_ref[1, m]
        power = term if power is None else power + term
    wide0 = jnp.concatenate([power, jnp.zeros_like(power)], axis=1)
    for s in range(nsets):

        def step(slot, carry, s=s):
            row = scals[s][slot] + s * strip
            col = scals[s][16 + slot]
            tile = jnp.minimum(col // 128, tiles - 2)
            wide = pltpu.roll(wide0, col - tile * 128, 1)
            for k in range(2):
                acc[tile + k, pl.ds(row, length), :] += wide[:, k * 128 : (k + 1) * 128]
            return carry

        lax.fori_loop(0, scals[s][32], step, 0)
    wait_all(copies)

    def combine(t, carry):
        share = 1.0 / (acc[t, first : first + rows] + 1.0)
        share_ref[t] = share
        for part in range(2):
            pre_ref[part, t] = frame[part, t] - grad[part, t] * share
        return carry

    lax.fori_loop(0, tiles, combine, 0)


def light(scalars, probe, objects, grads, strip, tiles, first, rows):
    natural = len(objects) == 3
    nsets = len(scalars)
    return pl.pallas_call(
        functools.partial(light_kernel, nsets, strip, first, natural),
        out_shape=(f32(2, tiles, rows, 128), f32(tiles, rows, 128)),
        in_specs=[smem()] * nsets + [anywhere()] * (1 + len(objects) + len(grads)),
        out_specs=(vmem(), vmem()),
        scratch_shapes=[
            pltpu.VMEM((tiles, (nsets + 1) * strip, 128), jnp.float32),
            pltpu.VMEM((2, tiles, rows, 128), jnp.float32),
            pltpu.VMEM((2, tiles, rows, 128), jnp.float32),
            pltpu.VMEM(probe.shape, jnp.float32),
            pltpu.SemaphoreType.DMA((3, tiles)),
            pltpu.SemaphoreType.DMA((5,)),
        ],
        compiler_params=pltpu.CompilerParams(vmem_limit_bytes=VMEM_LIMIT),
        cost_estimate=pl.CostEstimate(flops=1000, bytes_accessed=1000, transcendentals=0),
        name="light",
    )(*scalars, probe, *objects, *grads)


def meet_kernel(scal_ref, pre, share, cross, chip, out):
    strip = cross.shape[2]
    core = scal_ref[PLACE - 1]

    def tile(t, carry):
        for part in range(2):
            for k, got in ((core, cross), (1 - core, chip)):
                r = pl.ds(pl.multiple_of(k * strip, 8), strip)
                out[part, t, r, :] = pre[part, t, r, :] - got[part, t] * share[t, r, :]
        return carry

    lax.fori_loop(0, out.shape[1], tile, 0)


def meet(scalars, pre, share, cross, chip):
    return pl.pallas_call(
        meet_kernel,
        out_shape=f32(*pre.shape),
        in_specs=[smem()] + [vmem()] * 4,
        out_specs=vmem(),
        compiler_params=pltpu.CompilerParams(vmem_limit_bytes=VMEM_LIMIT),
        cost_estimate=pl.CostEstimate(flops=1000, bytes_accessed=1000, transcendentals=0),
        name="meet",
    )(scalars, pre, share, cross, chip)


def last_kernel(scal_ref, pre, share, cross, chip, out):
    half = cross.shape[2]
    core = scal_ref[PLACE - 1]
    for t in range(pre.shape[1]):
        c = slice(t * 128, (t + 1) * 128)
        for part in range(2):
            for k, got in ((core, cross), (1 - core, chip)):
                r = pl.ds(pl.multiple_of(k * half, 8), half)
                out[part, r, c] = pre[part, t, r, :] - got[part, t] * share[t, r, :]


def last(scalars, pre, share, cross, chip):
    tiles, strip = pre.shape[1:3]

    def block(rows):
        return pl.BlockSpec((2, STEP_TILES, rows, 128), lambda j: (0, j, 0, 0))

    return pl.pallas_call(
        last_kernel,
        out_shape=f32(2, strip, tiles * 128),
        grid=(tiles // STEP_TILES,),
        in_specs=[smem(), block(strip), pl.BlockSpec((STEP_TILES, strip, 128), lambda j: (j, 0, 0)), block(strip // 2), block(strip // 2)],
        out_specs=pl.BlockSpec((2, strip, STEP_TILES * 128), lambda j: (0, 0, j)),
        compiler_params=pltpu.CompilerParams(vmem_limit_bytes=VMEM_LIMIT),
        cost_estimate=pl.CostEstimate(flops=1000, bytes_accessed=1000, transcendentals=0),
        name="last",
    )(scalars, pre, share, cross, chip)


def shift_by(value, steps):
    count = lax.axis_size("dev")
    return lax.ppermute(
        value, "dev", [(i, i + steps) for i in range(count) if 0 <= i + steps < count]
    )


def rotate(value, stride, extent, steps):
    count = lax.axis_size("dev")

    def target(i):
        z = (i // stride) % extent
        return i + ((z + steps) % extent - z) * stride

    return lax.ppermute(value, "dev", [(i, target(i)) for i in range(count)])


def small_call(kernel, out_shape, operands, scratch=()):
    several = isinstance(out_shape, tuple)
    return pl.pallas_call(
        kernel,
        out_shape=out_shape,
        in_specs=[smem()] + [vmem()] * (len(operands) - 1),
        out_specs=(vmem(),) * len(out_shape) if several else vmem(),
        scratch_shapes=list(scratch),
        compiler_params=pltpu.CompilerParams(vmem_limit_bytes=8 * MIB),
        cost_estimate=pl.CostEstimate(flops=1000, bytes_accessed=1000, transcendentals=0),
        name=kernel.__name__,
    )(*operands)


def deal_kernel(scal_ref, keep, got, *outs):
    rows = outs[0].shape[0]
    for k, out in enumerate(outs):
        r = pl.ds(pl.multiple_of(lax.rem(scal_ref[PLACE] + k, len(outs)) * rows, 8), rows)
        out[...] = keep[r, :] + got[r, :]


def gather_kernel(scal_ref, *refs):
    pieces, out = refs[:-1], refs[-1]
    rows, count = pieces[0].shape[0], len(pieces)
    for k, piece in zip((0,) + TURNS, pieces):
        r = pl.ds(pl.multiple_of(lax.rem(scal_ref[PLACE] + count - k, count) * rows, 8), rows)
        out[r, :] = piece[...]


def probe_kernel(scal_ref, mine, other, probe, out, summed):
    half = mine.shape[0]
    core = scal_ref[PLACE - 1]
    summed[pl.ds(pl.multiple_of(core * half, 8), half), :] = mine[...]
    summed[pl.ds(pl.multiple_of((1 - core) * half, 8), half), :] = other[...]
    parts, nmodes, length = probe.shape[:3]
    share = 1.0 / (summed[parts * nmodes * length :, :] + 1.0)
    for part in range(parts):
        for m in range(nmodes):
            first = (part * nmodes + m) * length
            out[part, m] = probe[part, m] - summed[first : first + length, :] * share


def ring_sum(own, pieces, stride):
    total = own
    for k in TURNS:
        total = total + rotate(pieces[k - 1], stride, 4, k)
    return total


def shards(object_field, probe, amplitudes, positions, counts):
    strip, columns = object_field.shape[1:]
    nmodes, length = probe.shape[1], probe.shape[-1]
    half, tiles = strip // 2, columns // 128
    barrier = lax.optimization_barrier
    device = lax.axis_index("dev")
    mine = jnp.concatenate([positions[:, 0] - device * strip, positions[:, 1], counts, (device % 2)[None], (device // 32 % 4)[None]])

    def scattered(keep, send):
        pieces = small_call(deal_kernel, (f32(keep.shape[0] // 4, length),) * 4, (mine, keep, rotate(send, 1, 2, 1)))
        return ring_sum(pieces[0], pieces[1:], 32)

    def gathered(part):
        part = ring_sum(part, (part,) * 3, 2)
        pieces = [part] + [rotate(part, 32, 4, k) for k in TURNS]
        return small_call(gather_kernel, f32(4 * part.shape[0], length), [mine] + pieces)

    def moved(probe, half):
        terms = pltpu.VMEM((2 * half.shape[0], length), jnp.float32)
        return small_call(probe_kernel, f32(*probe.shape), (mine, half, rotate(half, 1, 2, 1), probe), (terms,))

    core = device % 2
    count = lax.axis_size("dev")
    chip_down = [(i, i + 1) for i in range(0, count, 2)]
    cross_down = [(i, i + 1) for i in range(1, count - 1, 2)]

    def swap(value, pairs):
        return lax.ppermute(value, "dev", pairs + [(j, i) for i, j in pairs])

    def exchange(cross, chip):
        return swap(cross, cross_down), swap(chip, chip_down)

    extra = jnp.pad(mine.astype(jnp.float32)[None, None], ((0, 1), (0, 7), (0, columns - mine.shape[0])))

    def edge(which):
        return jnp.concatenate([lax.dynamic_slice_in_dim(object_field, which * half, half, 1), extra], axis=1)

    def info(halo):
        return halo[0, half, : mine.shape[0]].astype(jnp.int32)

    cross, chip = exchange(edge(core), edge(1 - core))
    amps_cross = lax.ppermute(amplitudes, "dev", cross_down)
    amps_chip = swap(amplitudes, chip_down)
    second = shift_by(mine, 2)
    from_chip = info(chip)
    amps = (amplitudes, amps_chip)
    before = patterns("first", (mine, jnp.where(core == 0, mine, from_chip)), (chip, object_field), None, amps, probe, tiles, 1000)
    second, cross, amps_cross, before = barrier((second, cross, amps_cross, before))
    from_cross = info(cross)
    chosen = jnp.where(core == 0, from_cross, mine)
    amps = (amplitudes, amps_cross)
    out, inner, keep, send = patterns("second", (mine, chosen), (cross, object_field), before, amps, probe, tiles, 10**9)
    got, got_inner = exchange(out, inner)
    prev = jnp.where(core == 0, from_cross, from_chip)
    following = jnp.where(core == 0, from_chip, from_cross)
    near = (second, prev, mine, following)
    pre, share = light(near, probe, (cross, chip, object_field), (out, inner), strip, tiles, strip + half, 2 * strip)
    got, got_inner, pre, share, part = barrier((got, got_inner, pre, share, scattered(keep, send)))
    frame, part = barrier((meet(mine, pre, share, got, got_inner), ring_sum(part, (part,) * 3, 8)))
    probe = moved(probe, gathered(part))

    amps = (amplitudes, amps_chip, amps_cross)
    out, inner, gmid, keep, send = patterns("both", (mine, prev), (frame,), None, amps, probe, tiles, 10**9)
    got, got_inner = exchange(out, inner)
    pre, share = light((prev, mine), probe, (frame,), (gmid,), strip, tiles, strip, strip)
    got, got_inner, pre, share, part = barrier((got, got_inner, pre, share, scattered(keep, send)))
    current, part = barrier((last(mine, pre, share, got, got_inner), ring_sum(part, (part,) * 3, 8)))
    return (current, moved(probe, gathered(part)))


def solution(mesh):
    placed = (P(None, "dev", None), P(), P("dev", None, None), P("dev", None), P("dev"))
    return jax.shard_map(
        shards, mesh=mesh, in_specs=placed, out_specs=(P(None, "dev", None), P()), check_vma=False
    )
```
